256 devices in a mesh: lon: 4 (over x_lo, core), lat: 64 (over y, x_hi, z).
Axes of the slice: x: 4 (x_hi: 2, x_lo: 2; x = x_hi * 2 + x_lo), y: 4, z: 8, core: 2. Of those that a mesh axis runs over, the one named last changes fastest.
Arguments:
- tokens: bfloat16 [2, 384, 192, 512], P(None, 'lat', 'lon'), may hold values from -6 to 6
- cotangent: bfloat16 [2, 384, 192, 512], P(None, 'lat', 'lon'), may hold values from -6 to 6
- norm_gain: float32 [512], replicated, may hold values from 0.5 to 1.5
- qkv_weight: bfloat16 [512, 1536], replicated
- out_weight: bfloat16 [512, 512], replicated, may hold values from -0.25 to 0.25
Outputs:
- layer_out: bfloat16 [2, 384, 192, 512], P(None, 'lat', 'lon')
- grad_tokens: bfloat16 [2, 384, 192, 512], P(None, 'lat', 'lon')
- grad_qkv: float32 [512, 1536], replicated
- grad_out: float32 [512, 512], replicated
- grad_gain: float32 [512], replicated
The draws below stay inside these ranges and needn't reach their ends.
All inputs are finite; a program needn't handle non-finite values.
Results may differ from the reference program's by a relative error of at most 0.0097.
Values may be sent and summed in bfloat16 or wider, within the bound.
A program may use at most 64 MiB of HBM per device.

```python
import jax
import jax.numpy as jnp
from jax import lax

D = 512
HEADS = 8
LEVELS = 2
WIN_LAT = 6
WIN_LON = 12
NLAT = 384
NLON = 192
TOKENS = 147456


def draw_qkv_weight(key, part):
    key = jax.random.fold_in(key, 11)
    first_key = jax.random.fold_in(key, 0)
    return (jax.random.normal(first_key, (D, 3 * D), jnp.float32) * D ** (-0.5)).astype(jnp.bfloat16)


def block_scale(key, dims, shards, smallest, high):
    def one(axis_at, blocks):
        heights = jax.random.uniform(jax.random.fold_in(jax.random.fold_in(key, 6), axis_at), (blocks,), jnp.float32, smallest / len(shards), high / len(shards))
        return jnp.repeat(jnp.exp(heights), dims[axis_at] // blocks).reshape((-1,) + (1,) * (len(dims) - axis_at - 1))

    level = one(*shards[0])
    for cut in shards[1:]:
        level = level * one(*cut)
    return level


def gaussian(own_key, dims, deviation, bound, cuts=(), kind=jnp.bfloat16):
    values = deviation * jax.random.normal(own_key, dims, jnp.float32)
    if cuts:
        values = values * block_scale(own_key, dims, cuts, -0.22, 0.18)
    return jnp.clip(values, -bound, bound).astype(kind)


def setup_inputs(seed: int = 0) -> dict:
    arg_keys = jax.random.split(jax.random.key(seed), 6)
    tokens = gaussian(arg_keys[0], (LEVELS, NLAT, NLON, D), 1.0, 6.0, ((1, 64), (2, 4)))
    cotangent = gaussian(arg_keys[1], (LEVELS, NLAT, NLON, D), 1.0, 6.0, ((1, 64), (2, 4)))
    norm_gain = jnp.clip(1.0 + 0.1 * jax.random.normal(arg_keys[2], (D,), jnp.float32), 0.5, 1.5)
    qkv_weight = draw_qkv_weight(jax.random.fold_in(arg_keys[5], 71), 0)
    out_weight = gaussian(arg_keys[4], (D, D), D ** -0.5, 0.25)
    return {"tokens": tokens, "cotangent": cotangent, "norm_gain": norm_gain, "qkv_weight": qkv_weight, "out_weight": out_weight}


EPSILON = 1e-05

def widen(array):
    return array.astype(jnp.float32)

def norm_parts(tokens):
    widened = widen(tokens)
    centre = lax.optimization_barrier(jnp.mean(widened, -1, keepdims=True))
    spread = widened - centre
    inv_std = lax.rsqrt(lax.optimization_barrier(jnp.mean(spread * spread, -1, keepdims=True)) + EPSILON)
    return (widened, spread * inv_std, inv_std)

def to_windows(field_grid):
    levels, lat_rows, lon_cols, feat_width = field_grid.shape
    pieces = field_grid.reshape(levels, lat_rows // WIN_LAT, WIN_LAT, lon_cols // WIN_LON, WIN_LON, feat_width)
    pieces = pieces.transpose(1, 3, 0, 2, 4, 5)
    return pieces.reshape(-1, levels * WIN_LAT * WIN_LON, feat_width)

def from_windows(stacked, levels, lat_rows, lon_cols):
    feat_width = stacked.shape[-1]
    pieces = stacked.reshape(lat_rows // WIN_LAT, lon_cols // WIN_LON, levels, WIN_LAT, WIN_LON, feat_width)
    return pieces.transpose(2, 0, 3, 1, 4, 5).reshape(levels, lat_rows, lon_cols, feat_width)

def allowed_pairs(window_flags, win_span):
    offset = jnp.arange(win_span) // WIN_LON % WIN_LAT
    upper_half = offset < WIN_LAT // 2
    same_half = upper_half[:, None] == upper_half[None, :]
    return same_half[None, None] | jnp.logical_not(window_flags)[:, None, None, None]

def attend_forward(tok_windows, qkv_weight, window_flags, head_count):
    win_count, win_span, feat_width = tok_windows.shape
    head_dim = feat_width // head_count
    score_scale = head_dim ** (-0.5)
    qkv_rows = jnp.einsum('bsd,de->bse', widen(tok_windows), widen(qkv_weight)).astype(jnp.bfloat16)
    queries = qkv_rows[..., :feat_width].reshape(win_count, win_span, head_count, head_dim)
    keys_part = qkv_rows[..., feat_width:2 * feat_width].reshape(win_count, win_span, head_count, head_dim)
    values_part = qkv_rows[..., 2 * feat_width:].reshape(win_count, win_span, head_count, head_dim)
    scores = jnp.einsum('bqhe,bkhe->bhqk', widen(queries), widen(keys_part)) * score_scale
    scores = jnp.where(allowed_pairs(window_flags, win_span), scores, -1e+30)
    row_peak = lax.optimization_barrier(jnp.max(scores, -1, keepdims=True))
    exp_scores = jnp.exp(scores - row_peak)
    attn_probs = (exp_scores / lax.optimization_barrier(jnp.sum(exp_scores, -1, keepdims=True))).astype(jnp.bfloat16)
    attn_mixed = jnp.einsum('bhqk,bkhe->bqhe', widen(attn_probs), widen(values_part))
    attn_mixed = attn_mixed.astype(jnp.bfloat16).reshape(win_count, win_span, feat_width)
    return (qkv_rows, attn_probs, attn_mixed)

def attend_backward(tok_windows, cot_windows, qkv_rows, attn_probs, attn_mixed, qkv_weight, out_weight, head_count):
    win_count, win_span, feat_width = tok_windows.shape
    head_dim = feat_width // head_count
    score_scale = head_dim ** (-0.5)
    queries = qkv_rows[..., :feat_width].reshape(win_count, win_span, head_count, head_dim)
    keys_part = qkv_rows[..., feat_width:2 * feat_width].reshape(win_count, win_span, head_count, head_dim)
    values_part = qkv_rows[..., 2 * feat_width:].reshape(win_count, win_span, head_count, head_dim)
    grad_mixed = jnp.einsum('bse,de->bsd', widen(cot_windows), widen(out_weight)).astype(jnp.bfloat16)
    wout_part = jnp.einsum('bsd,bse->de', widen(attn_mixed), widen(cot_windows))
    grad_heads = grad_mixed.reshape(win_count, win_span, head_count, head_dim)
    grad_values = jnp.einsum('bhqk,bqhe->bkhe', widen(attn_probs), widen(grad_heads))
    grad_probs = jnp.einsum('bqhe,bkhe->bhqk', widen(grad_heads), widen(values_part))
    probs_wide = widen(attn_probs)
    row_total = lax.optimization_barrier(jnp.sum(grad_probs * probs_wide, -1, keepdims=True))
    grad_scores = (probs_wide * (grad_probs - row_total) * score_scale).astype(jnp.bfloat16)
    grad_queries = jnp.einsum('bhqk,bkhe->bqhe', widen(grad_scores), widen(keys_part))
    grad_keys = jnp.einsum('bhqk,bqhe->bkhe', widen(grad_scores), widen(queries))
    grad_rows = jnp.concatenate([grad_queries.reshape(win_count, win_span, feat_width), grad_keys.reshape(win_count, win_span, feat_width), grad_values.reshape(win_count, win_span, feat_width)], -1).astype(jnp.bfloat16)
    qkv_part = jnp.einsum('bsd,bse->de', widen(tok_windows), widen(grad_rows))
    return (grad_rows, qkv_part, wout_part)

def reference(tokens, cotangent, norm_gain, qkv_weight, out_weight):
    widened, normal_x, inv_std = norm_parts(tokens)
    normed = (normal_x * norm_gain).astype(jnp.bfloat16)
    shifted = jnp.roll(normed, (WIN_LAT // 2, WIN_LON // 2), axis=(1, 2))
    cot_shift = jnp.roll(cotangent, (WIN_LAT // 2, WIN_LON // 2), axis=(1, 2))
    win_span = LEVELS * WIN_LAT * WIN_LON
    lat_blocks = NLAT // WIN_LAT
    lon_blocks = NLON // WIN_LON
    tok_windows = to_windows(shifted).reshape(lat_blocks, lon_blocks, win_span, D)
    cot_windows = to_windows(cot_shift).reshape(lat_blocks, lon_blocks, win_span, D)

    def block_step(running, inputs):
        tok_block, cot_block, block_index = inputs
        window_flags = jnp.full((lon_blocks,), block_index == 0)
        qkv_rows, attn_probs, attn_mixed = attend_forward(tok_block, qkv_weight, window_flags, HEADS)
        proj_rows = jnp.einsum('bsd,de->bse', widen(attn_mixed), widen(out_weight)).astype(jnp.bfloat16)
        grad_rows, qkv_part, wout_part = attend_backward(tok_block, cot_block, qkv_rows, attn_probs, attn_mixed, qkv_weight, out_weight, HEADS)
        grad_windows = jnp.einsum('bse,de->bsd', widen(grad_rows), widen(qkv_weight)).astype(jnp.bfloat16)
        return ((running[0] + qkv_part, running[1] + wout_part), (proj_rows, grad_windows))
    start = (jnp.zeros((D, 3 * D), jnp.float32), jnp.zeros((D, D), jnp.float32))
    sums, outputs = lax.scan(block_step, start, (tok_windows, cot_windows, jnp.arange(lat_blocks, dtype=jnp.int32)))
    proj_grid = from_windows(outputs[0].reshape(-1, win_span, D), LEVELS, NLAT, NLON)
    grad_grid = from_windows(outputs[1].reshape(-1, win_span, D), LEVELS, NLAT, NLON)
    proj_grid = jnp.roll(proj_grid, (-(WIN_LAT // 2), -(WIN_LON // 2)), axis=(1, 2))
    grad_normed = jnp.roll(grad_grid, (-(WIN_LAT // 2), -(WIN_LON // 2)), axis=(1, 2))
    layer_out = (widened + widen(proj_grid)).astype(jnp.bfloat16)
    grad_wide = widen(grad_normed)
    gain_part = lax.optimization_barrier(jnp.sum(grad_wide * normal_x, axis=(0, 1, 2)))
    scaled = grad_wide * norm_gain
    grad_tokens = widen(cotangent) + inv_std * (scaled - lax.optimization_barrier(jnp.mean(scaled, -1, keepdims=True)) - normal_x * lax.optimization_barrier(jnp.mean(scaled * normal_x, -1, keepdims=True)))
    grad_tokens = grad_tokens.astype(jnp.bfloat16)
    factor = 1.0 / jnp.sqrt(jnp.float32(TOKENS))
    return (layer_out, grad_tokens, sums[0] * factor, sums[1] * factor, gain_part * factor)
```

```python
import jax
import jax.numpy as jnp
import numpy as np
from jax import lax
from jax.experimental import pallas as pl
from jax.experimental.pallas import tpu as pltpu
from jax.sharding import PartitionSpec as P

MESH = pl.DeviceIdType.MESH
F32 = jnp.float32
BF16 = jnp.bfloat16
EPSILON = 1e-05
D = 512
SPAN = 144
HALF = 72
LEVELS, LATS, LONS = 2, 6, 48
RING = {"x": 4, "y": 4, "z": 8}

RUNS = ((0, 6, 0), (6, 12, 48), (18, 12, 128), (30, 12, 208), (42, 6, 288))
PACKED = 336
UL, LL, LR, UR, S1U, S1L, S2U, S3U, S2L, S3L = 0, 48, 96, 144, 192, 272, 352, 432, 512, 592
STAGED = 672
BASES = (0, 192, 352, 416)


def packing():
    table = np.zeros((PACKED, LEVELS * 3 * LONS), np.float32)
    for first, width, row in RUNS:
        for level in range(LEVELS):
            for lat in range(3):
                for lon in range(width):
                    table[row, (level * 3 + lat) * LONS + first + lon] = 1
                    row += 1
    return table


def gathering():
    table = np.zeros((4, SPAN, 256), np.float32)
    quarter = LEVELS * 3 * 6
    for at, start in enumerate((UL, UR, LL, LR)):
        for row in range(quarter):
            table[0, at * quarter + row, start + row] = 1
    for slot, starts in ((1, (S1U, S1L)), (2, (S2U, S2L)), (3, (S3U, S3L))):
        for at, start in enumerate(starts):
            for row in range(HALF):
                table[slot, at * HALF + row, start - BASES[slot] + row] = 1
    return table


def scattering():
    gather = gathering()
    table = np.zeros((STAGED, 4 * SPAN), np.float32)
    for slot in range(4):
        table[BASES[slot] : BASES[slot] + 256, slot * SPAN : (slot + 1) * SPAN] += gather[slot].T
    return table


def dot(a, b):
    return jnp.dot(a, b, preferred_element_type=F32)


def dot_nt(a, b):
    return lax.dot_general(a, b, (((1,), (1,)), ((), ())), preferred_element_type=F32)


def dot_tn(a, b):
    return lax.dot_general(a, b, (((0,), (0,)), ((), ())), preferred_element_type=F32)


def place():
    lat, lon = lax.axis_index("lat"), lax.axis_index("lon")
    return {"x": lon // 2 + 2 * ((lat // 8) % 2), "y": lat // 16, "z": lat % 8, "core": lon % 2}


def device(at):
    return {"lat": (at["y"] * 2 + at["x"] // 2) * 8 + at["z"], "lon": (at["x"] % 2) * 2 + at["core"]}


def moved(axis, steps):
    at = place()
    if axis == "core":
        at["core"] = 1 - at["core"]
    else:
        at[axis] = (at[axis] + steps + RING[axis]) % RING[axis]
    return device(at)


def grid_moved(lat_steps, lon_steps):
    lat, lon = lax.axis_index("lat"), lax.axis_index("lon")
    return {"lat": (lat + lat_steps + 64) % 64, "lon": (lon + lon_steps + 4) % 4}


def kernel(
    tok_ref, cot_ref, gain_ref, wqkv_ref, wout_ref, pack_ref, unpack_ref, gather_ref, scatter_ref,
    lay_ref, gtok_ref, gqkv_ref, gout_ref, ggain_ref,
    packed, staged, back, arrived, xhat_s, inv_s, tokw, normed, cotw, qkv, gmix, mixed, grows,
    send0, recv0, acc0, send1, recv1, acc1, send2, recv2, send3, recv3, full3, full1, other,
    gain_own, gain_core, gain_x, gain_y, gain_z,
    halo_s, halo_r, back_s, back_r, s0, r0, s1, r1, s2, r2, s3, r3, s4, r4, s5, r5, s6, r6, s7, r7, sg, rg,
):
    pending = []

    def remote(src, dst, send_sem, recv_sem, target):
        return pltpu.make_async_remote_copy(
            src_ref=src, dst_ref=dst, send_sem=send_sem, recv_sem=recv_sem, device_id=target, device_id_type=MESH
        )

    def begin(copy):
        copy.start()
        pending.append(copy)
        return copy

    barrier = pltpu.get_barrier_semaphore()
    friends = [grid_moved(1, 0), grid_moved(-1, 0), grid_moved(0, 1), grid_moved(0, -1), grid_moved(1, 1), grid_moved(-1, -1)]
    friends.append(moved("core", 1))
    for axis in ("x", "y", "z"):
        friends += [moved(axis, step) for step in range(1, RING[axis])]
    for friend in friends:
        pl.semaphore_signal(barrier, inc=1, device_id=friend, device_id_type=MESH)

    me = place()
    lat = lax.axis_index("lat")

    for at, source in enumerate((tok_ref, cot_ref)):
        for half in range(2):
            rows = source[:, 3 * half : 3 * half + 3].reshape(LEVELS * 3 * LONS, D)
            packed[at, half] = dot(pack_ref[...], rows).astype(BF16)
        staged[at, LR : LR + 48] = packed[at, 0, 0:48]
        staged[at, S1L : S1L + 80] = packed[at, 0, 48:128]
        staged[at, S2U : S2U + 160] = packed[at, 1, 128:288]

    pl.semaphore_wait(barrier, len(friends))

    def halo(at):
        routes = (
            (packed.at[at, 1, pl.ds(0, 128)], staged.at[at, pl.ds(UR, 128)], grid_moved(1, 0)),
            (packed.at[at, 0, pl.ds(128, 160)], staged.at[at, pl.ds(S2L, 160)], grid_moved(-1, 0)),
            (packed.at[at, 0, pl.ds(288, 48)], staged.at[at, pl.ds(LL, 48)], grid_moved(0, 1)),
            (packed.at[at, 1, pl.ds(288, 48)], staged.at[at, pl.ds(UL, 48)], grid_moved(1, 1)),
        )
        return [
            begin(remote(src, dst, halo_s.at[at, n], halo_r.at[at, n], target))
            for n, (src, dst, target) in enumerate(routes)
        ]

    tok_halo = halo(0)
    cot_halo = halo(1)
    for copy in tok_halo:
        copy.wait_recv()

    for slot in range(4):
        rows = pl.ds(slot * SPAN, SPAN)
        x = dot(gather_ref[slot], staged[0, BASES[slot] : BASES[slot] + 256])
        tokw[rows] = x.astype(BF16)
        spread = x - jnp.mean(x, -1, keepdims=True)
        inv_std = lax.rsqrt(jnp.mean(spread * spread, -1, keepdims=True) + EPSILON)
        xhat = spread * inv_std
        xhat_s[rows] = xhat
        inv_s[rows] = inv_std
        normed[rows] = (xhat * gain_ref[...]).astype(BF16)

    for part in range(3):
        columns = pl.ds(part * D, D)
        qkv[:, columns] = dot(normed[...], wqkv_ref[:, columns]).astype(BF16)

    for copy in cot_halo:
        copy.wait_recv()
    for slot in range(4):
        rows = pl.ds(slot * SPAN, SPAN)
        cotw[rows] = dot(gather_ref[slot], staged[1, BASES[slot] : BASES[slot] + 256]).astype(BF16)
    gmix[...] = dot_nt(cotw[...], wout_ref[...]).astype(BF16)

    low_lanes = lax.broadcasted_iota(jnp.int32, (SPAN, 128), 1) < 64
    apart = (lax.broadcasted_iota(jnp.int32, (SPAN, SPAN), 0) < HALF) != (
        lax.broadcasted_iota(jnp.int32, (SPAN, SPAN), 1) < HALF
    )

    def stack(block):
        zero = jnp.zeros_like(block)
        return jnp.concatenate([jnp.where(low_lanes, block, zero), jnp.where(low_lanes, zero, block)], 0)

    def unstack(block):
        return jnp.where(low_lanes, block[:SPAN], block[SPAN:])

    def window(slot, _):
        rows = pl.ds(pl.multiple_of(slot * SPAN, SPAN), SPAN)
        cut = ((slot < 2) & (lat == 0)) | ((slot >= 2) & (lat == 63))
        bias = jnp.where(apart & cut, -1e30, 0.0)
        for pair in range(4):
            lanes = pl.ds(pair * 128, 128)
            q = qkv[rows, lanes]
            k = stack(qkv[rows, pl.ds(D + pair * 128, 128)])
            v = stack(qkv[rows, pl.ds(2 * D + pair * 128, 128)])
            gm = gmix[rows, lanes]
            scores = dot_nt(k, q).reshape(2, SPAN, SPAN) + bias
            peak = jnp.max(scores, 1, keepdims=True)
            weights = jnp.exp2((scores - peak) * (0.125 * 1.4426950408889634))
            probs = weights * (1.0 / jnp.sum(weights, 1, keepdims=True))
            probs = probs.astype(BF16)
            flat = probs.reshape(2 * SPAN, SPAN)
            mixed[rows, lanes] = dot_tn(flat, v).astype(BF16)
            gprobs = dot_nt(v, gm).reshape(2, SPAN, SPAN)
            wide = probs.astype(F32)
            total = jnp.sum(wide * gprobs, 1, keepdims=True)
            gscores = (wide * (gprobs - total)).astype(BF16).reshape(2 * SPAN, SPAN)
            grows[rows, lanes] = (dot_tn(gscores, k) * 0.125).astype(BF16)
            grows[rows, pl.ds(D + pair * 128, 128)] = (unstack(dot(gscores, q)) * 0.125).astype(BF16)
            grows[rows, pl.ds(2 * D + pair * 128, 128)] = unstack(dot(flat, gm)).astype(BF16)
        return 0

    lax.fori_loop(0, 4, window, 0)

    orders = (("x", "y"), ("y", "x"), ("x", "y"), ("y", "x"))
    pair_copies = []
    for group in range(4):
        if group < 3:
            total = dot_tn(normed[...], grows[:, group * D : (group + 1) * D])
        else:
            total = dot_tn(mixed[...], cotw[...])
        total = [total[:, n * 128 : (n + 1) * 128].reshape(32, 16, 128) for n in range(4)]
        first = me["core"] == 0
        for n in range(2):
            acc0[group, n * 32 : (n + 1) * 32] = jnp.where(first, total[n], total[n + 2])
            send0[group, n * 32 : (n + 1) * 32] = jnp.where(first, total[n + 2], total[n]).astype(BF16)
        pair_copies.append(begin(remote(send0.at[group], recv0.at[group], s0.at[group], r0.at[group], moved("core", 1))))

    def give_back(at, values):
        back[at] = dot(scatter_ref[...], values).astype(BF16)
        arrived[at, 0, 0:48] = back[at, LR : LR + 48]
        arrived[at, 0, 48:128] = back[at, S1L : S1L + 80]
        arrived[at, 1, 128:288] = back[at, S2U : S2U + 160]
        routes = (
            (back.at[at, pl.ds(UR, 128)], arrived.at[at, 1, pl.ds(0, 128)], grid_moved(-1, 0)),
            (back.at[at, pl.ds(S2L, 160)], arrived.at[at, 0, pl.ds(128, 160)], grid_moved(1, 0)),
            (back.at[at, pl.ds(LL, 48)], arrived.at[at, 0, pl.ds(288, 48)], grid_moved(0, -1)),
            (back.at[at, pl.ds(UL, 48)], arrived.at[at, 1, pl.ds(288, 48)], grid_moved(-1, -1)),
        )
        return [
            begin(remote(src, dst, back_s.at[at, n], back_r.at[at, n], target))
            for n, (src, dst, target) in enumerate(routes)
        ]

    def take_back(at, copies, out):
        for copy in copies:
            copy.wait_recv()
        for half in range(2):
            rows = dot(unpack_ref[...], arrived[at, half]).astype(BF16)
            out[:, 3 * half : 3 * half + 3] = rows.reshape(LEVELS, 3, LONS, D)

    first_copies = []
    for group in range(4):
        axis = orders[group][0]
        pair_copies[group].wait_recv()
        acc0[group] = acc0[group] + recv0[group].astype(F32)
        send1[group] = acc0[group].astype(BF16)
        for step in range(1, 4):
            shard = (me[axis] + step) % 4
            first_copies.append(begin(remote(
                send1.at[group, pl.ds(shard * 16, 16)], recv1.at[group, step - 1],
                s1.at[group, step - 1], r1.at[group, step - 1], moved(axis, step),
            )))

    proj = dot(mixed[...], wout_ref[...]).astype(BF16)
    lay_copies = give_back(0, (tokw[...].astype(F32) + proj.astype(F32)).astype(BF16))

    gnormed = dot_nt(grows[...], wqkv_ref[...]).astype(BF16).astype(F32)
    xhat = xhat_s[...]
    gain_rows = jnp.sum(gnormed * xhat, 0, keepdims=True)
    gain_own[...] = jnp.concatenate(
        [gain_rows[:, n * 128 : (n + 1) * 128] for n in range(4)] + [jnp.zeros((4, 128), F32)], 0
    )
    gain_copies = [begin(remote(gain_own, gain_core, sg.at[0], rg.at[0], moved("core", 1)))]
    scaled = gnormed * gain_ref[...]
    gtok = cotw[...].astype(F32) + inv_s[...] * (
        scaled - jnp.mean(scaled, -1, keepdims=True) - xhat * jnp.mean(scaled * xhat, -1, keepdims=True)
    )
    gtok_copies = give_back(1, gtok.astype(BF16))

    second_copies = []
    for group in range(4):
        first, axis = orders[group]
        for copy in first_copies[group * 3 : group * 3 + 3]:
            copy.wait_recv()
        total = acc0[group, pl.ds(me[first] * 16, 16)]
        for step in range(3):
            total = total + recv1[group, step].astype(F32)
        acc1[group] = total
        send2[group] = total.astype(BF16)
        for step in range(1, 4):
            shard = (me[axis] + step) % 4
            second_copies.append(begin(remote(
                send2.at[group, pl.ds(shard * 4, 4)], recv2.at[group, step - 1],
                s2.at[group, step - 1], r2.at[group, step - 1], moved(axis, step),
            )))

    gain_copies[0].wait_recv()
    gain_x[0] = gain_own[...] + gain_core[...]
    for step in range(1, 4):
        gain_copies.append(begin(remote(gain_x.at[0], gain_x.at[step], sg.at[step], rg.at[step], moved("x", step))))

    third_copies = []
    for group in range(4):
        axis = orders[group][1]
        for copy in second_copies[group * 3 : group * 3 + 3]:
            copy.wait_recv()
        total = acc1[group, pl.ds(me[axis] * 4, 4)]
        for step in range(3):
            total = total + recv2[group, step].astype(F32)
        send3[group] = total.reshape(8, 8, 128)
        for step in range(1, 8):
            shard = (me["z"] + step) % 8
            third_copies.append(begin(remote(
                send3.at[group, shard], recv3.at[group, step - 1],
                s3.at[group, step - 1], r3.at[group, step - 1], moved("z", step),
            )))

    for copy in gain_copies[1:4]:
        copy.wait_recv()
    gain_y[0] = gain_x[0] + gain_x[1] + gain_x[2] + gain_x[3]
    for step in range(1, 4):
        gain_copies.append(begin(remote(gain_y.at[0], gain_y.at[step], sg.at[3 + step], rg.at[3 + step], moved("y", step))))

    factor = 1.0 / np.sqrt(np.float32(147456))
    fourth_copies = []
    for group in range(4):
        for copy in third_copies[group * 7 : group * 7 + 7]:
            copy.wait_recv()
        total = send3[group, me["z"]]
        for step in range(7):
            total = total + recv3[group, step]
        full3[group, me["z"]] = total * factor
        own = full3.at[group, me["z"]]
        for step in range(1, 8):
            fourth_copies.append(begin(remote(own, own, s4.at[group, step - 1], r4.at[group, step - 1], moved("z", step))))

    for copy in gain_copies[4:7]:
        copy.wait_recv()
    gain_z[0] = gain_y[0] + gain_y[1] + gain_y[2] + gain_y[3]
    for step in range(1, 8):
        gain_copies.append(begin(remote(gain_z.at[0], gain_z.at[step], sg.at[6 + step], rg.at[6 + step], moved("z", step))))

    def received(copy_of, axis, step):
        return copy_of((me[axis] + RING[axis] - step) % RING[axis], step)

    def z_copy(group):
        return lambda at, step: remote(
            full3.at[group, at], full3.at[group, at], s4.at[group, step - 1], r4.at[group, step - 1], moved("z", step)
        )

    def second_copy(group):
        first, axis = orders[group]

        def copy_of(at, step):
            block = full1.at[group, pl.ds(me[first] * 16 + at * 4, 4)]
            return remote(block, block, s5.at[group, step - 1], r5.at[group, step - 1], moved(axis, step))

        return copy_of

    def first_copy(group):
        axis = orders[group][0]

        def copy_of(at, step):
            block = full1.at[group, pl.ds(at * 16, 16)]
            return remote(block, block, s6.at[group, step - 1], r6.at[group, step - 1], moved(axis, step))

        return copy_of

    for group in range(4):
        first, axis = orders[group]
        for step in range(1, 8):
            received(z_copy(group), "z", step).wait_recv()
        at = me[first] * 16 + me[axis] * 4
        full1[group, pl.ds(at, 4)] = full3[group].reshape(4, 16, 128).astype(BF16)
        for step in range(1, 4):
            begin(second_copy(group)(me[axis], step))

    for group in range(4):
        first, axis = orders[group]
        for step in range(1, 4):
            received(second_copy(group), axis, step).wait_recv()
        for step in range(1, 4):
            begin(first_copy(group)(me[first], step))

    take_back(0, lay_copies, lay_ref)
    take_back(1, gtok_copies, gtok_ref)

    for copy in gain_copies[7:]:
        copy.wait_recv()
    total = gain_z[0]
    for step in range(1, 8):
        total = total + gain_z[step]
    ggain_ref[...] = total * factor

    last_copies = []
    for group in range(4):
        for step in range(1, 4):
            received(first_copy(group), orders[group][0], step).wait_recv()
        last_copies.append(begin(remote(full1.at[group], other.at[group], s7.at[group], r7.at[group], moved("core", 1))))

    for group in range(4):
        last_copies[group].wait_recv()
        first = me["core"] == 0
        for n in range(2):
            mine = full1[group, n * 32 : (n + 1) * 32].astype(F32).reshape(512, 128)
            theirs = other[group, n * 32 : (n + 1) * 32].astype(F32).reshape(512, 128)
            low, high = jnp.where(first, mine, theirs), jnp.where(first, theirs, mine)
            for at, value in ((n, low), (n + 2, high)):
                if group < 3:
                    gqkv_ref[:, group * D + at * 128 : group * D + (at + 1) * 128] = value
                else:
                    gout_ref[:, at * 128 : (at + 1) * 128] = value

    for copy in pending:
        copy.wait_send()


def on_device(tokens, cotangent, norm_gain, qkv_weight, out_weight):
    pack = packing()
    tables = [jnp.asarray(table, BF16) for table in (pack, pack.T, gathering(), scattering())]
    vmem = pl.BlockSpec(memory_space=pltpu.VMEM)
    dma = pltpu.SemaphoreType.DMA
    rows = 4 * SPAN
    scratch = [
        pltpu.VMEM((2, 2, PACKED, D), BF16),
        pltpu.VMEM((2, STAGED, D), BF16),
        pltpu.VMEM((2, STAGED, D), BF16),
        pltpu.VMEM((2, 2, PACKED, D), BF16),
        pltpu.VMEM((rows, D), F32),
        pltpu.VMEM((rows, 1), F32),
        pltpu.VMEM((rows, D), BF16),
        pltpu.VMEM((rows, D), BF16),
        pltpu.VMEM((rows, D), BF16),
        pltpu.VMEM((rows, 3 * D), BF16),
        pltpu.VMEM((rows, D), BF16),
        pltpu.VMEM((rows, D), BF16),
        pltpu.VMEM((rows, 3 * D), BF16),
        pltpu.VMEM((4, 64, 16, 128), BF16),
        pltpu.VMEM((4, 64, 16, 128), BF16),
        pltpu.VMEM((4, 64, 16, 128), F32),
        pltpu.VMEM((4, 64, 16, 128), BF16),
        pltpu.VMEM((4, 3, 16, 16, 128), BF16),
        pltpu.VMEM((4, 16, 16, 128), F32),
        pltpu.VMEM((4, 16, 16, 128), BF16),
        pltpu.VMEM((4, 3, 4, 16, 128), BF16),
        pltpu.VMEM((4, 8, 8, 128), F32),
        pltpu.VMEM((4, 7, 8, 128), F32),
        pltpu.VMEM((4, 8, 8, 128), F32),
        pltpu.VMEM((4, 64, 16, 128), BF16),
        pltpu.VMEM((4, 64, 16, 128), BF16),
        pltpu.VMEM((8, 128), F32),
        pltpu.VMEM((8, 128), F32),
        pltpu.VMEM((4, 8, 128), F32),
        pltpu.VMEM((4, 8, 128), F32),
        pltpu.VMEM((8, 8, 128), F32),
        dma((2, 4)), dma((2, 4)), dma((2, 4)), dma((2, 4)),
        dma((4,)), dma((4,)),
        dma((4, 3)), dma((4, 3)),
        dma((4, 3)), dma((4, 3)),
        dma((4, 7)), dma((4, 7)),
        dma((4, 7)), dma((4, 7)),
        dma((4, 3)), dma((4, 3)),
        dma((4, 3)), dma((4, 3)),
        dma((4,)), dma((4,)),
        dma((14,)), dma((14,)),
    ]
    layer_out, grad_tokens, grad_qkv, grad_out, grad_gain = pl.pallas_call(
        kernel,
        out_shape=(
            jax.ShapeDtypeStruct(tokens.shape, BF16),
            jax.ShapeDtypeStruct(tokens.shape, BF16),
            jax.ShapeDtypeStruct((D, 3 * D), F32),
            jax.ShapeDtypeStruct((D, D), F32),
            jax.ShapeDtypeStruct((8, 128), F32),
        ),
        in_specs=[vmem] * 9,
        out_specs=(vmem,) * 5,
        scratch_shapes=scratch,
        compiler_params=pltpu.CompilerParams(
            collective_id=0, has_side_effects=True, vmem_limit_bytes=56 * 1024 * 1024
        ),
        name="sublayer",
    )(tokens, cotangent, norm_gain.reshape(1, D), qkv_weight, out_weight, *tables)
    return layer_out, grad_tokens, grad_qkv, grad_out, grad_gain[:4].reshape(D)


def solution(mesh):
    grid = P(None, "lat", "lon", None)
    return jax.shard_map(
        on_device,
        mesh=mesh,
        in_specs=(grid, grid, P(), P(), P()),
        out_specs=(grid, grid, P(), P(), P()),
        check_vma=False,
    )
```

```python
import jax
import jax.numpy as jnp
import numpy as np
from jax import lax
from jax.experimental import pallas as pl
from jax.experimental.pallas import tpu as pltpu
from jax.sharding import PartitionSpec as P

MESH = pl.DeviceIdType.MESH
F32 = jnp.float32
BF16 = jnp.bfloat16
EPSILON = 1e-05
D = 512
SPAN = 144
HALF = 72
LEVELS, LATS, LONS = 2, 6, 48
RING = {"x": 4, "y": 4, "z": 8}

RUNS = ((0, 6, 0), (6, 12, 48), (18, 12, 128), (30, 12, 208), (42, 6, 288))
PACKED = 336
UL, LL, LR, UR, S1U, S1L, S2U, S3U, S2L, S3L = 0, 48, 96, 144, 192, 272, 352, 432, 512, 592
STAGED = 672
BASES = (0, 192, 336, 416)
AT_ONCE = (2, 3)


def packing():
    table = np.zeros((PACKED, LEVELS * 3 * LONS), np.float32)
    for first, width, row in RUNS:
        for level in range(LEVELS):
            for lat in range(3):
                for lon in range(width):
                    table[row, (level * 3 + lat) * LONS + first + lon] = 1
                    row += 1
    return table


def gathering():
    table = np.zeros((4, SPAN, 256), np.float32)
    quarter = LEVELS * 3 * 6
    for at, start in enumerate((UL, UR, LL, LR)):
        for row in range(quarter):
            table[0, at * quarter + row, start + row] = 1
    for slot, starts in ((1, (S1U, S1L)), (2, (S2U, S2L)), (3, (S3U, S3L))):
        for at, start in enumerate(starts):
            for row in range(HALF):
                table[slot, at * HALF + row, start - BASES[slot] + row] = 1
    return table


def scattering():
    gather = gathering()
    table = np.zeros((STAGED, 4 * SPAN), np.float32)
    for slot in range(4):
        table[BASES[slot] : BASES[slot] + 256, slot * SPAN : (slot + 1) * SPAN] += gather[slot].T
    return table


def dot(a, b):
    return jnp.dot(a, b, preferred_element_type=F32)


def dot_nt(a, b):
    return lax.dot_general(a, b, (((1,), (1,)), ((), ())), preferred_element_type=F32)


def dot_tn(a, b):
    return lax.dot_general(a, b, (((0,), (0,)), ((), ())), preferred_element_type=F32)


def place():
    lat, lon = lax.axis_index("lat"), lax.axis_index("lon")
    return {"x": (lon >> 1) + 2 * ((lat >> 3) & 1), "y": lat >> 4, "z": lat & 7, "core": lon & 1}


def device(at):
    return {"lat": at["y"] * 16 + (at["x"] >> 1) * 8 + at["z"], "lon": (at["x"] & 1) * 2 + at["core"]}


def targets():
    found = {("core", 1): device(dict(place(), core=1 - place()["core"]))}
    for axis, size in RING.items():
        for step in range(1, size):
            at = place()
            at[axis] = (at[axis] + step) & (size - 1)
            found[axis, step] = device(at)
    lat, lon = lax.axis_index("lat"), lax.axis_index("lon")
    for steps in ((1, 0), (-1, 0), (0, 1), (0, -1), (1, 1), (-1, -1)):
        found[steps] = {"lat": (lat + steps[0]) & 63, "lon": (lon + steps[1]) & 3}
    return found


def kernel(
    tok_hbm, cot_hbm, gain_ref, wqkv_hbm, wout_hbm, pack_hbm, unpack_hbm, gather_hbm, scatter_hbm,
    lay_ref, gtok_ref, grads_ref, ggain_ref,
    tok_ref, cot_ref, wqkv_ref, wout_ref, pack_ref, unpack_ref, gather_ref, scatter_ref, out_s,
    packed, staged, back, arrived, xhat_s, inv_s, tokw, normed, cotw, qkv, gmix, probs_s, mixed, grows,
    send0, recv0, acc0, send1, recv1, acc1, send2, recv2, send3, recv3, full3, all3, full1,
    gain_own, gain_core, gain_x, gain_y, gain_z,
    local_s, halo_s, halo_r, back_s, back_r,
    s0, r0, s1, r1, s2, r2, s3, r3, s4, r4, s5, r5, s6, r6, s7, r7, sg, rg,
):
    pending = []
    locals_out = []

    def remote(src, dst, send_sem, recv_sem, target):
        return pltpu.make_async_remote_copy(
            src_ref=src, dst_ref=dst, send_sem=send_sem, recv_sem=recv_sem, device_id=target, device_id_type=MESH
        )

    def begin(copy):
        copy.start()
        pending.append(copy)
        return copy

    barrier = pltpu.get_barrier_semaphore()
    known = targets()
    friends = list(known.values())

    def moved(axis, step):
        return known[axis, step]

    grid_moved = moved
    loads = {}
    for at, (name, src, dst) in enumerate((
        ("tok", tok_hbm, tok_ref), ("pack", pack_hbm, pack_ref), ("cot", cot_hbm, cot_ref), ("gather", gather_hbm, gather_ref),
        ("wqkv", wqkv_hbm, wqkv_ref), ("wout", wout_hbm, wout_ref), ("scatter", scatter_hbm, scatter_ref), ("unpack", unpack_hbm, unpack_ref),
    )):
        loads[name] = pltpu.make_async_copy(src, dst, local_s.at[at])
        if at < 2:
            loads[name].start()
    for friend in friends:
        pl.semaphore_signal(barrier, inc=1, device_id=friend, device_id_type=MESH)
    for name in ("cot", "gather", "wqkv", "wout", "scatter", "unpack"):
        loads[name].start()

    me = place()
    lat = lax.axis_index("lat")

    def prepare(at, source):
        for half in range(2):
            rows = source[:, 3 * half : 3 * half + 3].reshape(LEVELS * 3 * LONS, D)
            packed[at, half] = dot(pack_ref[...], rows).astype(BF16)
        staged[at, LR : LR + 48] = packed[at, 0, 0:48]
        staged[at, S1L : S1L + 80] = packed[at, 0, 48:128]
        staged[at, S2U : S2U + 160] = packed[at, 1, 128:288]

    def halo(at):
        routes = (
            (packed.at[at, 1, pl.ds(48, 80)], staged.at[at, pl.ds(S1U, 80)], grid_moved(1, 0)),
            (packed.at[at, 0, pl.ds(128, 80)], staged.at[at, pl.ds(S2L, 80)], grid_moved(-1, 0)),
            (packed.at[at, 1, pl.ds(0, 48)], staged.at[at, pl.ds(UR, 48)], grid_moved(1, 0)),
            (packed.at[at, 0, pl.ds(208, 80)], staged.at[at, pl.ds(S3L, 80)], grid_moved(-1, 0)),
            (packed.at[at, 0, pl.ds(288, 48)], staged.at[at, pl.ds(LL, 48)], grid_moved(0, 1)),
            (packed.at[at, 1, pl.ds(288, 48)], staged.at[at, pl.ds(UL, 48)], grid_moved(1, 1)),
        )
        return [
            begin(remote(src, dst, halo_s.at[at, n], halo_r.at[at, n], target))
            for n, (src, dst, target) in enumerate(routes)
        ]

    loads["tok"].wait()
    loads["pack"].wait()
    prepare(0, tok_ref)
    pl.semaphore_wait(barrier, len(friends))
    tok_halo = halo(0)
    loads["cot"].wait()
    prepare(1, cot_ref)
    loads["gather"].wait()
    loads["wqkv"].wait()
    def enter(slot):
        rows = pl.ds(slot * SPAN, SPAN)
        x = dot(gather_ref[slot], staged[0, BASES[slot] : BASES[slot] + 256])
        tokw[rows] = x.astype(BF16)
        spread = x - jnp.mean(x, -1, keepdims=True)
        inv_std = lax.rsqrt(jnp.mean(spread * spread, -1, keepdims=True) + EPSILON)
        xhat = spread * inv_std
        xhat_s[rows] = xhat
        inv_s[rows] = inv_std
        normed[rows] = (xhat * gain_ref[...]).astype(BF16)

    def project(first, second):
        rows = jnp.concatenate([normed[slot * SPAN : (slot + 1) * SPAN] for slot in (first, second)], 0)
        for part in range(3):
            columns = pl.ds(part * D, D)
            both = dot(rows, wqkv_ref[:, columns]).astype(BF16)
            qkv[first * SPAN : (first + 1) * SPAN, columns] = both[:SPAN]
            qkv[second * SPAN : (second + 1) * SPAN, columns] = both[SPAN:]

    low_lanes = lax.broadcasted_iota(jnp.int32, (SPAN, 128), 1) < 64
    apart = (lax.broadcasted_iota(jnp.int32, (SPAN, SPAN), 0) < HALF) != (
        lax.broadcasted_iota(jnp.int32, (SPAN, SPAN), 1) < HALF
    )

    def stack(block):
        zero = jnp.zeros_like(block)
        return jnp.concatenate([jnp.where(low_lanes, block, zero), jnp.where(low_lanes, zero, block)], 0)

    def unstack(block):
        return jnp.where(low_lanes, block[:SPAN], block[SPAN:])

    def rows_of(slot):
        return pl.ds(pl.multiple_of(slot * SPAN, SPAN), SPAN)

    def columns_of(part, pair):
        return pl.ds(part * D + pair * 128, 128)

    def forward(slot, _):
        rows = rows_of(slot)
        cut = ((slot < 2) & (lat == 0)) | ((slot >= 2) & (lat == 63))
        bias = jnp.where(apart & cut, -1e30, 0.0)
        for pair in range(4):
            k = stack(qkv[rows, columns_of(1, pair)])
            scores = dot_nt(k, qkv[rows, columns_of(0, pair)]).reshape(2, SPAN, SPAN) + bias
            peak = jnp.max(scores, 1, keepdims=True)
            weights = jnp.exp2((scores - peak) * (0.125 * 1.4426950408889634))
            probs = weights * (1.0 / jnp.sum(weights, 1, keepdims=True))
            probs = probs.astype(BF16).reshape(2 * SPAN, SPAN)
            probs_s[slot * 4 + pair] = probs
            mixed[rows, columns_of(0, pair)] = dot_tn(probs, stack(qkv[rows, columns_of(2, pair)])).astype(BF16)
        return 0

    for copy in tok_halo[:2]:
        copy.wait_recv()
    cot_halo = halo(1)
    enter(1)
    enter(2)
    project(1, 2)
    lax.fori_loop(0, 2, lambda at, carry: forward(at + 1, carry), 0)
    for copy in tok_halo[2:]:
        copy.wait_recv()
    enter(0)
    enter(3)
    project(0, 3)
    lax.fori_loop(0, 2, lambda at, carry: forward(at * 3, carry), 0)

    loads["wout"].wait()
    for copy in cot_halo:
        copy.wait_recv()
    for slot in range(4):
        rows = pl.ds(slot * SPAN, SPAN)
        cotw[rows] = dot(gather_ref[slot], staged[1, BASES[slot] : BASES[slot] + 256]).astype(BF16)
    gmix[...] = dot_nt(cotw[...], wout_ref[...]).astype(BF16)

    orders = (("x", "y"), ("y", "x"), ("x", "y"), ("y", "x"))
    factor = 1.0 / np.sqrt(np.float32(147456))
    copies = {}
    first_core = me["core"] == 0

    def reduce_pair(group):
        columns = jnp.concatenate([grows[:, part * D + group * 128 : part * D + (group + 1) * 128] for part in range(3)], 1)
        total = dot_tn(normed[...], columns)
        rows = dot_tn(mixed[:, group * 128 : (group + 1) * 128], cotw[...])
        total = [total[:, n * 128 : (n + 1) * 128].reshape(32, 16, 128) for n in range(3)]
        total.append(jnp.concatenate([rows[:, n * 128 : (n + 1) * 128].reshape(8, 16, 128) for n in range(4)], 0))
        for n in range(2):
            acc0[group, n * 32 : (n + 1) * 32] = jnp.where(first_core, total[n], total[n + 2])
            send0[group, n * 32 : (n + 1) * 32] = jnp.where(first_core, total[n + 2], total[n]).astype(BF16)
        copies[0, group] = [begin(remote(send0.at[group], recv0.at[group], s0.at[group], r0.at[group], moved("core", 1)))]

    def settle(phase, group):
        for copy in copies[phase, group]:
            copy.wait_recv()

    def reduce_first(group):
        axis = orders[group][0]
        settle(0, group)
        acc0[group] = acc0[group] + recv0[group].astype(F32)
        send1[group] = acc0[group].astype(BF16)
        copies[1, group] = []
        for step in (2, 1, 3):
            shard = (me[axis] + step) & 3
            copies[1, group].append(begin(remote(
                send1.at[group, pl.ds(shard * 16, 16)], recv1.at[group, step - 1],
                s1.at[group, step - 1], r1.at[group, step - 1], moved(axis, step),
            )))

    def reduce_second(group):
        first, axis = orders[group]
        settle(1, group)
        total = acc0[group, pl.ds(me[first] * 16, 16)]
        for step in range(3):
            total = total + recv1[group, step].astype(F32)
        acc1[group] = total
        send2[group] = total.astype(BF16)
        copies[2, group] = []
        for step in (2, 1, 3):
            shard = (me[axis] + step) & 3
            copies[2, group].append(begin(remote(
                send2.at[group, pl.ds(shard * 4, 4)], recv2.at[group, step - 1],
                s2.at[group, step - 1], r2.at[group, step - 1], moved(axis, step),
            )))

    def reduce_third(group):
        axis = orders[group][1]
        settle(2, group)
        total = acc1[group, pl.ds(me[axis] * 4, 4)]
        for step in range(3):
            total = total + recv2[group, step].astype(F32)
        copies[3, group] = []
        if group in AT_ONCE:
            part = all3.at[group, me["z"]]
            part[...] = (total * factor).astype(BF16)
            for step in (4, 3, 5, 2, 6, 1, 7):
                begin(remote(part, part, s3.at[group, step - 1], r3.at[group, step - 1], moved("z", step)))
            return
        send3[group] = total.reshape(8, 8, 128)
        for step in (4, 3, 5, 2, 6, 1, 7):
            shard = (me["z"] + step) & 7
            copies[3, group].append(begin(remote(
                send3.at[group, shard], recv3.at[group, step - 1],
                s3.at[group, step - 1], r3.at[group, step - 1], moved("z", step),
            )))

    def spread_third(group):
        settle(3, group)
        total = send3[group, me["z"]]
        for step in range(7):
            total = total + recv3[group, step]
        full3[group, me["z"]] = total * factor
        own = full3.at[group, me["z"]]
        for step in (4, 3, 5, 2, 6, 1, 7):
            begin(remote(own, own, s4.at[group, step - 1], r4.at[group, step - 1], moved("z", step)))

    def sender(axis, step):
        return (me[axis] + RING[axis] - step) & (RING[axis] - 1)

    def spread_second(group):
        first, axis = orders[group]
        own = pl.ds(me[first] * 16 + me[axis] * 4, 4)
        buffer, sent, came = (all3, s3, r3) if group in AT_ONCE else (full3, s4, r4)
        for step in (1, 7, 2, 6, 3, 5, 4):
            block = buffer.at[group, sender("z", step)]
            remote(block, block, sent.at[group, step - 1], came.at[group, step - 1], moved("z", step)).wait_recv()
        if group in AT_ONCE:
            total = all3[group, 0].astype(F32)
            for at in range(1, 8):
                total = total + all3[group, at].astype(F32)
            full1[group, own] = total.astype(BF16)
        else:
            full1[group, own] = full3[group].reshape(4, 16, 128).astype(BF16)
        block = full1.at[group, own]
        for step in (2, 1, 3):
            begin(remote(block, block, s5.at[group, step - 1], r5.at[group, step - 1], moved(axis, step)))

    def spread_first(group):
        first, axis = orders[group]
        for step in range(1, 4):
            block = full1.at[group, pl.ds(me[first] * 16 + sender(axis, step) * 4, 4)]
            remote(block, block, s5.at[group, step - 1], r5.at[group, step - 1], moved(axis, step)).wait_recv()
        block = full1.at[group, pl.ds(me[first] * 16, 16)]
        for step in (2, 1, 3):
            begin(remote(block, block, s6.at[group, step - 1], r6.at[group, step - 1], moved(first, step)))
        to_pair(group, me[first], 0)

    def to_pair(group, shard, step):
        rows = pl.ds(shard * 16, 16)
        begin(remote(
            full1.at[group, rows], grads_ref.at[group, me["core"], rows], s7.at[group, step], r7.at[group, step], moved("core", 1)
        ))

    def spread_pair(group):
        axis = orders[group][0]
        for step in (1, 3, 2):
            block = full1.at[group, pl.ds(sender(axis, step) * 16, 16)]
            remote(block, block, s6.at[group, step - 1], r6.at[group, step - 1], moved(axis, step)).wait_recv()
            to_pair(group, sender(axis, step), step)
        keep = pltpu.make_async_copy(full1.at[group], grads_ref.at[group, me["core"]], local_s.at[8 + group])
        keep.start()
        locals_out.append(keep)

    def finish_pair(group):
        axis = orders[group][0]
        for step in range(4):
            rows = pl.ds(sender(axis, step) * 16, 16)
            remote(
                full1.at[group, rows], grads_ref.at[group, 1 - me["core"], rows], s7.at[group, step], r7.at[group, step], moved("core", 1)
            ).wait_recv()

    def give_back(at, values):
        back[at] = dot(scatter_ref[...], values).astype(BF16)
        arrived[at, 0, 0:48] = back[at, LR : LR + 48]
        arrived[at, 0, 48:128] = back[at, S1L : S1L + 80]
        arrived[at, 1, 128:288] = back[at, S2U : S2U + 160]
        routes = (
            (back.at[at, pl.ds(UR, 128)], arrived.at[at, 1, pl.ds(0, 128)], grid_moved(-1, 0)),
            (back.at[at, pl.ds(S2L, 160)], arrived.at[at, 0, pl.ds(128, 160)], grid_moved(1, 0)),
            (back.at[at, pl.ds(LL, 48)], arrived.at[at, 0, pl.ds(288, 48)], grid_moved(0, -1)),
            (back.at[at, pl.ds(UL, 48)], arrived.at[at, 1, pl.ds(288, 48)], grid_moved(-1, -1)),
        )
        return [
            begin(remote(src, dst, back_s.at[at, n], back_r.at[at, n], target))
            for n, (src, dst, target) in enumerate(routes)
        ]

    def take_back(at, arriving, out):
        for copy in arriving:
            copy.wait_recv()
        for half in range(2):
            rows = dot(unpack_ref[...], arrived[at, half]).astype(BF16)
            out_s[at, :, 3 * half : 3 * half + 3] = rows.reshape(LEVELS, 3, LONS, D)
        keep = pltpu.make_async_copy(out_s.at[at], out, local_s.at[12 + at])
        keep.start()
        locals_out.append(keep)

    def gain_copy(src, dst, sem, axis, step):
        return remote(src, dst, sg.at[sem], rg.at[sem], moved(axis, step))

    def gain_send(axis, buffer, value, first):
        own = buffer.at[me[axis]]
        own[...] = value
        for step in range(1, RING[axis]):
            begin(gain_copy(own, own, first + step, axis, step))

    def gain_take(axis, buffer, first):
        for step in range(1, RING[axis]):
            block = buffer.at[sender(axis, step)]
            gain_copy(block, block, first + step, axis, step).wait_recv()
        total = buffer[0]
        for at in range(1, RING[axis]):
            total = total + buffer[at]
        return total

    def backward(pair):
        def two_windows(half, _):
            for slot in (2 * half, 2 * half + 1):
                rows = rows_of(slot)
                probs = probs_s[slot * 4 + pair]
                gm = gmix[rows, columns_of(0, pair)]
                grows[rows, columns_of(2, pair)] = unstack(dot(probs, gm)).astype(BF16)
                gprobs = dot_nt(stack(qkv[rows, columns_of(2, pair)]), gm).reshape(2, SPAN, SPAN)
                wide = probs.astype(F32).reshape(2, SPAN, SPAN)
                total = jnp.sum(wide * gprobs, 1, keepdims=True)
                gscores = (wide * (gprobs - total)).astype(BF16).reshape(2 * SPAN, SPAN)
                grows[rows, columns_of(0, pair)] = (dot_tn(gscores, stack(qkv[rows, columns_of(1, pair)])) * 0.125).astype(BF16)
                grows[rows, columns_of(1, pair)] = (unstack(dot(gscores, qkv[rows, columns_of(0, pair)])) * 0.125).astype(BF16)
            return 0

        lax.fori_loop(0, 2, two_windows, 0)

    proj = dot(mixed[...], wout_ref[...]).astype(BF16)
    loads["scatter"].wait()
    lay_copies = give_back(0, (tokw[...].astype(F32) + proj.astype(F32)).astype(BF16))
    backward(0)
    reduce_pair(0)
    backward(1)
    reduce_pair(1)
    reduce_first(0)
    backward(2)
    reduce_pair(2)
    reduce_first(1)
    backward(3)
    reduce_pair(3)
    reduce_first(2)
    gnormed = dot_nt(grows[...], wqkv_ref[...]).astype(BF16).astype(F32)
    reduce_first(3)
    reduce_second(0)
    xhat = xhat_s[...]
    gain_rows = jnp.sum(gnormed * xhat, 0, keepdims=True)
    gain_own[...] = jnp.concatenate(
        [gain_rows[:, n * 128 : (n + 1) * 128] for n in range(4)] + [jnp.zeros((4, 128), F32)], 0
    )
    begin(gain_copy(gain_own, gain_core, 0, "core", 1))
    scaled = gnormed * gain_ref[...]
    gtok = cotw[...].astype(F32) + inv_s[...] * (
        scaled - jnp.mean(scaled, -1, keepdims=True) - xhat * jnp.mean(scaled * xhat, -1, keepdims=True)
    )
    reduce_second(1)
    gtok_copies = give_back(1, gtok.astype(BF16))
    reduce_second(2)
    reduce_third(0)
    gain_copy(gain_own, gain_core, 0, "core", 1).wait_recv()
    gain_send("x", gain_x, gain_own[...] + gain_core[...], 0)
    reduce_second(3)
    reduce_third(1)
    reduce_third(2)
    gain_send("y", gain_y, gain_take("x", gain_x, 0), 3)
    loads["unpack"].wait()
    take_back(0, lay_copies, lay_ref)
    spread_third(0)
    reduce_third(3)
    spread_third(1)
    gain_send("z", gain_z, gain_take("y", gain_y, 3), 6)
    take_back(1, gtok_copies, gtok_ref)
    for group in (2, 0, 3, 1):
        spread_second(group)
    for group in (2, 0, 3, 1):
        spread_first(group)
    ggain_ref[...] = gain_take("z", gain_z, 6) * factor
    for group in (2, 0, 3, 1):
        spread_pair(group)
    for group in (2, 0, 3, 1):
        finish_pair(group)
    for copy in locals_out:
        copy.wait()
    for copy in pending:
        copy.wait_send()


def unpack_kernel(lay_in, gtok_in, grads_in, gain_in, lay_out, gtok_out, gqkv_out, gout_out, gain_out, narrow, wide, last, grids, sems):
    moves = [pltpu.make_async_copy(grads_in.at[group], narrow.at[group], sems.at[group]) for group in range(4)]
    moves += [pltpu.make_async_copy(source, grids.at[at], sems.at[4 + at]) for at, source in enumerate((lay_in, gtok_in))]
    outs = []
    for at in (4, 5, 0, 1, 2, 3):
        moves[at].start()
    for n in range(4):
        gain_out[:, n * 128 : (n + 1) * 128] = gain_in[n : n + 1]
    for at, target in enumerate((lay_out, gtok_out)):
        moves[4 + at].wait()
        outs.append(pltpu.make_async_copy(grids.at[at], target, sems.at[10 + at]))
        outs[-1].start()
    for group in range(4):
        moves[group].wait()
        for part in range(3):
            tiles = narrow[group, part // 2, (part % 2) * 32 : (part % 2 + 1) * 32]
            columns = pl.ds(part * D + group * 128, 128)
            wide[:, columns] = tiles.astype(F32).reshape(D, 128)
            outs.append(pltpu.make_async_copy(wide.at[:, columns], gqkv_out.at[:, columns], sems.at[12 + group * 3 + part]))
            outs[-1].start()
        for n in range(4):
            tiles = narrow[group, 1, 32 + n * 8 : 32 + (n + 1) * 8]
            last[group * 128 : (group + 1) * 128, n * 128 : (n + 1) * 128] = tiles.astype(F32).reshape(128, 128)
        rows = pl.ds(group * 128, 128)
        outs.append(pltpu.make_async_copy(last.at[rows], gout_out.at[rows], sems.at[6 + group]))
        outs[-1].start()
    for copy in outs:
        copy.wait()


def on_device(tokens, cotangent, norm_gain, qkv_weight, out_weight):
    pack = packing()
    tables = [jnp.asarray(table, BF16) for table in (pack, pack.T, gathering(), scattering())]
    vmem = pl.BlockSpec(memory_space=pltpu.VMEM)
    anywhere = pl.BlockSpec(memory_space=pl.ANY)
    dma = pltpu.SemaphoreType.DMA
    rows = 4 * SPAN
    scratch = [
        pltpu.VMEM(tokens.shape, BF16),
        pltpu.VMEM(tokens.shape, BF16),
        pltpu.VMEM((D, 3 * D), BF16),
        pltpu.VMEM((D, D), BF16),
        *[pltpu.VMEM(table.shape, BF16) for table in tables],
        pltpu.VMEM((2, *tokens.shape), BF16),
        pltpu.VMEM((2, 2, PACKED, D), BF16),
        pltpu.VMEM((2, STAGED, D), BF16),
        pltpu.VMEM((2, STAGED, D), BF16),
        pltpu.VMEM((2, 2, PACKED, D), BF16),
        pltpu.VMEM((rows, D), F32),
        pltpu.VMEM((rows, 1), F32),
        pltpu.VMEM((rows, D), BF16),
        pltpu.VMEM((rows, D), BF16),
        pltpu.VMEM((rows, D), BF16),
        pltpu.VMEM((rows, 3 * D), BF16),
        pltpu.VMEM((rows, D), BF16),
        pltpu.VMEM((16, 2 * SPAN, SPAN), BF16),
        pltpu.VMEM((rows, D), BF16),
        pltpu.VMEM((rows, 3 * D), BF16),
        pltpu.VMEM((4, 64, 16, 128), BF16),
        pltpu.VMEM((4, 64, 16, 128), BF16),
        pltpu.VMEM((4, 64, 16, 128), F32),
        pltpu.VMEM((4, 64, 16, 128), BF16),
        pltpu.VMEM((4, 3, 16, 16, 128), BF16),
        pltpu.VMEM((4, 16, 16, 128), F32),
        pltpu.VMEM((4, 16, 16, 128), BF16),
        pltpu.VMEM((4, 3, 4, 16, 128), BF16),
        pltpu.VMEM((4, 8, 8, 128), F32),
        pltpu.VMEM((4, 7, 8, 128), F32),
        pltpu.VMEM((4, 8, 8, 128), F32),
        pltpu.VMEM((4, 8, 4, 16, 128), BF16),
        pltpu.VMEM((4, 64, 16, 128), BF16),
        pltpu.VMEM((8, 128), F32),
        pltpu.VMEM((8, 128), F32),
        pltpu.VMEM((4, 8, 128), F32),
        pltpu.VMEM((4, 8, 128), F32),
        pltpu.VMEM((8, 8, 128), F32),
        dma((14,)),
        dma((2, 6)), dma((2, 6)), dma((2, 4)), dma((2, 4)),
        dma((4,)), dma((4,)),
        dma((4, 3)), dma((4, 3)),
        dma((4, 3)), dma((4, 3)),
        dma((4, 7)), dma((4, 7)),
        dma((4, 7)), dma((4, 7)),
        dma((4, 3)), dma((4, 3)),
        dma((4, 3)), dma((4, 3)),
        dma((4, 4)), dma((4, 4)),
        dma((14,)), dma((14,)),
    ]
    grid = jax.ShapeDtypeStruct(tokens.shape, BF16)
    parts = pl.pallas_call(
        kernel,
        out_shape=(
            grid,
            grid,
            jax.ShapeDtypeStruct((4, 2, 64, 16, 128), BF16),
            jax.ShapeDtypeStruct((8, 128), F32),
        ),
        in_specs=[anywhere, anywhere, vmem] + [anywhere] * 6,
        out_specs=(anywhere, anywhere, anywhere, vmem),
        scratch_shapes=scratch,
        compiler_params=pltpu.CompilerParams(
            collective_id=0, has_side_effects=True, vmem_limit_bytes=56 * 1024 * 1024
        ),
        name="sublayer",
    )(tokens, cotangent, norm_gain.reshape(1, D), qkv_weight, out_weight, *tables)
    layer_out, grad_tokens, grad_qkv, grad_out, grad_gain = pl.pallas_call(
        unpack_kernel,
        out_shape=(
            grid,
            grid,
            jax.ShapeDtypeStruct((D, 3 * D), F32),
            jax.ShapeDtypeStruct((D, D), F32),
            jax.ShapeDtypeStruct((1, D), F32),
        ),
        in_specs=[anywhere] * 3 + [vmem],
        out_specs=(anywhere,) * 4 + (vmem,),
        scratch_shapes=[pltpu.VMEM((4, 2, 64, 16, 128), BF16), pltpu.VMEM((D, 3 * D), F32), pltpu.VMEM((D, D), F32), pltpu.VMEM((2, *tokens.shape), BF16), dma((24,))],
        compiler_params=pltpu.CompilerParams(vmem_limit_bytes=60 * 1024 * 1024),
        name="results",
    )(*parts)
    return layer_out, grad_tokens, grad_qkv, grad_out, grad_gain.reshape(D)


def solution(mesh):
    grid = P(None, "lat", "lon", None)
    return jax.shard_map(
        on_device,
        mesh=mesh,
        in_specs=(grid, grid, P(), P(), P()),
        out_specs=(grid, grid, P(), P(), P()),
        check_vma=False,
    )
```

```python
import jax
import jax.numpy as jnp
import numpy as np
from jax import lax
from jax.experimental import pallas as pl
from jax.experimental.pallas import tpu as pltpu
from jax.sharding import PartitionSpec as P

MESH = pl.DeviceIdType.MESH
F32 = jnp.float32
BF16 = jnp.bfloat16
EPSILON = 1e-05
D = 512
SPAN = 144
HALF = 72
LEVELS, LATS, LONS = 2, 6, 48
RING = {"x": 4, "y": 4, "z": 8}

RUNS = ((0, 6, 0), (6, 12, 48), (18, 12, 128), (30, 12, 208), (42, 6, 288))
PACKED = 336
UL, LL, LR, UR, S1U, S1L, S2U, S3U, S2L, S3L = 0, 48, 96, 144, 192, 272, 352, 432, 512, 592
STAGED = 672
BASES = (0, 192, 336, 416)


def packing():
    table = np.zeros((PACKED, LEVELS * 3 * LONS), np.float32)
    for first, width, row in RUNS:
        for level in range(LEVELS):
            for lat in range(3):
                for lon in range(width):
                    table[row, (level * 3 + lat) * LONS + first + lon] = 1
                    row += 1
    return table


def gathering():
    table = np.zeros((4, SPAN, 256), np.float32)
    quarter = LEVELS * 3 * 6
    for at, start in enumerate((UL, UR, LL, LR)):
        for row in range(quarter):
            table[0, at * quarter + row, start + row] = 1
    for slot, starts in ((1, (S1U, S1L)), (2, (S2U, S2L)), (3, (S3U, S3L))):
        for at, start in enumerate(starts):
            for row in range(HALF):
                table[slot, at * HALF + row, start - BASES[slot] + row] = 1
    return table


def scattering():
    gather = gathering()
    table = np.zeros((STAGED, 4 * SPAN), np.float32)
    for slot in range(4):
        table[BASES[slot] : BASES[slot] + 256, slot * SPAN : (slot + 1) * SPAN] += gather[slot].T
    return table


def dot(a, b):
    return jnp.dot(a, b, preferred_element_type=F32)


def dot_nt(a, b):
    return lax.dot_general(a, b, (((1,), (1,)), ((), ())), preferred_element_type=F32)


def dot_tn(a, b):
    return lax.dot_general(a, b, (((0,), (0,)), ((), ())), preferred_element_type=F32)


def place():
    lat, lon = lax.axis_index("lat"), lax.axis_index("lon")
    return {"x": (lon >> 1) + 2 * ((lat >> 3) & 1), "y": lat >> 4, "z": lat & 7, "core": lon & 1}


def device(at):
    return {"lat": at["y"] * 16 + (at["x"] >> 1) * 8 + at["z"], "lon": (at["x"] & 1) * 2 + at["core"]}


def targets():
    found = {("core", 1): device(dict(place(), core=1 - place()["core"]))}
    for axis, size in RING.items():
        for step in range(1, size):
            at = place()
            at[axis] = (at[axis] + step) & (size - 1)
            found[axis, step] = device(at)
    lat, lon = lax.axis_index("lat"), lax.axis_index("lon")
    for steps in ((1, 0), (-1, 0), (0, 1), (0, -1), (1, 1), (-1, -1)):
        found[steps] = {"lat": (lat + steps[0]) & 63, "lon": (lon + steps[1]) & 3}
    return found


def kernel(
    tok_hbm, cot_hbm, gain_ref, wqkv_hbm, wout_hbm, pack_hbm, unpack_hbm, gather_hbm, scatter_hbm,
    lay_ref, gtok_ref, grads_ref, ggain_ref,
    tok_ref, cot_ref, wqkv_ref, wout_ref, pack_ref, unpack_ref, gather_ref, scatter_ref, out_s,
    packed, staged, back, arrived, xhat_s, inv_s, tokw, normed, cotw, qkv, gmix, probs_s, mixed, grows,
    send0, recv0, acc0, send1, recv1, acc1, send2, recv2, acc2, send3, recv3, full3, full1,
    gain_own, gain_core, gain_x, gain_y, gain_z,
    local_s, halo_s, halo_r, back_s, back_r,
    s0, r0, s1, r1, s2, r2, s3, r3, s4, r4, s5, r5, s6, r6, s7, r7, sg, rg,
):
    pending = []
    locals_out = []

    def remote(src, dst, send_sem, recv_sem, target):
        return pltpu.make_async_remote_copy(
            src_ref=src, dst_ref=dst, send_sem=send_sem, recv_sem=recv_sem, device_id=target, device_id_type=MESH
        )

    def begin(copy):
        copy.start()
        pending.append(copy)
        return copy

    barrier = pltpu.get_barrier_semaphore()
    known = targets()
    friends = list(known.values())

    def moved(axis, step):
        return known[axis, step]

    grid_moved = moved
    loads = {}
    for at, (name, src, dst) in enumerate((
        ("tok", tok_hbm, tok_ref), ("pack", pack_hbm, pack_ref), ("cot", cot_hbm, cot_ref), ("gather", gather_hbm, gather_ref),
        ("wqkv", wqkv_hbm, wqkv_ref), ("wout", wout_hbm, wout_ref), ("scatter", scatter_hbm, scatter_ref), ("unpack", unpack_hbm, unpack_ref),
    )):
        loads[name] = pltpu.make_async_copy(src, dst, local_s.at[at])
        if at < 2:
            loads[name].start()
    for friend in friends:
        pl.semaphore_signal(barrier, inc=1, device_id=friend, device_id_type=MESH)
    for name in ("cot", "gather", "wqkv", "wout", "scatter", "unpack"):
        loads[name].start()

    me = place()
    lat = lax.axis_index("lat")

    def prepare(at, source):
        for half in range(2):
            rows = source[:, 3 * half : 3 * half + 3].reshape(LEVELS * 3 * LONS, D)
            packed[at, half] = dot(pack_ref[...], rows).astype(BF16)
        staged[at, LR : LR + 48] = packed[at, 0, 0:48]
        staged[at, S1L : S1L + 80] = packed[at, 0, 48:128]
        staged[at, S2U : S2U + 160] = packed[at, 1, 128:288]

    def halo(at):
        routes = (
            (packed.at[at, 1, pl.ds(48, 80)], staged.at[at, pl.ds(S1U, 80)], grid_moved(1, 0)),
            (packed.at[at, 0, pl.ds(128, 80)], staged.at[at, pl.ds(S2L, 80)], grid_moved(-1, 0)),
            (packed.at[at, 1, pl.ds(0, 48)], staged.at[at, pl.ds(UR, 48)], grid_moved(1, 0)),
            (packed.at[at, 0, pl.ds(208, 80)], staged.at[at, pl.ds(S3L, 80)], grid_moved(-1, 0)),
            (packed.at[at, 0, pl.ds(288, 48)], staged.at[at, pl.ds(LL, 48)], grid_moved(0, 1)),
            (packed.at[at, 1, pl.ds(288, 48)], staged.at[at, pl.ds(UL, 48)], grid_moved(1, 1)),
        )
        return [
            begin(remote(src, dst, halo_s.at[at, n], halo_r.at[at, n], target))
            for n, (src, dst, target) in enumerate(routes)
        ]

    loads["tok"].wait()
    loads["pack"].wait()
    prepare(0, tok_ref)
    pl.semaphore_wait(barrier, len(friends))
    tok_halo = halo(0)
    loads["cot"].wait()
    prepare(1, cot_ref)
    loads["gather"].wait()
    loads["wqkv"].wait()
    def enter(slot):
        rows = pl.ds(slot * SPAN, SPAN)
        x = dot(gather_ref[slot], staged[0, BASES[slot] : BASES[slot] + 256])
        tokw[rows] = x.astype(BF16)
        spread = x - jnp.mean(x, -1, keepdims=True)
        inv_std = lax.rsqrt(jnp.mean(spread * spread, -1, keepdims=True) + EPSILON)
        xhat = spread * inv_std
        xhat_s[rows] = xhat
        inv_s[rows] = inv_std
        normed[rows] = (xhat * gain_ref[...]).astype(BF16)

    def project(first, second):
        rows = jnp.concatenate([normed[slot * SPAN : (slot + 1) * SPAN] for slot in (first, second)], 0)
        for part in range(3):
            columns = pl.ds(part * D, D)
            both = dot(rows, wqkv_ref[:, columns]).astype(BF16)
            qkv[first * SPAN : (first + 1) * SPAN, columns] = both[:SPAN]
            qkv[second * SPAN : (second + 1) * SPAN, columns] = both[SPAN:]

    low_lanes = lax.broadcasted_iota(jnp.int32, (SPAN, 128), 1) < 64
    apart = (lax.broadcasted_iota(jnp.int32, (SPAN, SPAN), 0) < HALF) != (
        lax.broadcasted_iota(jnp.int32, (SPAN, SPAN), 1) < HALF
    )

    def stack(block):
        zero = jnp.zeros_like(block)
        return jnp.concatenate([jnp.where(low_lanes, block, zero), jnp.where(low_lanes, zero, block)], 0)

    def unstack(block):
        return jnp.where(low_lanes, block[:SPAN], block[SPAN:])

    def rows_of(slot):
        return pl.ds(slot * SPAN, SPAN)

    def columns_of(part, pair):
        return pl.ds(part * D + pair * 128, 128)

    def forward(slot):
        rows = rows_of(slot)
        cut = lat == (0 if slot < 2 else 63)
        bias = jnp.where(apart & cut, -1e30, 0.0)
        for pair in range(4):
            k = stack(qkv[rows, columns_of(1, pair)])
            scores = dot_nt(k, qkv[rows, columns_of(0, pair)]).reshape(2, SPAN, SPAN) + bias
            peak = jnp.max(scores, 1, keepdims=True)
            weights = jnp.exp2((scores - peak) * (0.125 * 1.4426950408889634))
            probs = weights * (1.0 / jnp.sum(weights, 1, keepdims=True))
            probs = probs.astype(BF16).reshape(2 * SPAN, SPAN)
            probs_s[slot * 4 + pair] = probs
            mixed[rows, columns_of(0, pair)] = dot_tn(probs, stack(qkv[rows, columns_of(2, pair)])).astype(BF16)

    for copy in tok_halo[:2]:
        copy.wait_recv()
    cot_halo = halo(1)
    enter(1)
    enter(2)
    project(1, 2)
    forward(1)
    forward(2)
    for copy in tok_halo[2:]:
        copy.wait_recv()
    enter(0)
    enter(3)
    project(0, 3)
    forward(0)
    forward(3)

    loads["wout"].wait()
    for copy in cot_halo:
        copy.wait_recv()
    for slot in range(4):
        rows = pl.ds(slot * SPAN, SPAN)
        cotw[rows] = dot(gather_ref[slot], staged[1, BASES[slot] : BASES[slot] + 256]).astype(BF16)
    gmix[...] = dot_nt(cotw[...], wout_ref[...]).astype(BF16)

    orders = (("x", "y"), ("y", "x"), ("x", "y"), ("y", "x"))
    factor = 1.0 / np.sqrt(np.float32(147456))
    copies = {}
    first_core = me["core"] == 0

    def reduce_pair(group):
        columns = jnp.concatenate([grows[:, part * D + group * 128 : part * D + (group + 1) * 128] for part in range(3)], 1)
        total = dot_tn(normed[...], columns)
        rows = dot_tn(mixed[:, group * 128 : (group + 1) * 128], cotw[...])
        total = [total[:, n * 128 : (n + 1) * 128].reshape(32, 16, 128) for n in range(3)]
        total.append(jnp.concatenate([rows[:, n * 128 : (n + 1) * 128].reshape(8, 16, 128) for n in range(4)], 0))
        for n in range(2):
            acc0[group, n * 32 : (n + 1) * 32] = jnp.where(first_core, total[n], total[n + 2])
            send0[group, n * 32 : (n + 1) * 32] = jnp.where(first_core, total[n + 2], total[n]).astype(BF16)
        copies[0, group] = [begin(remote(send0.at[group], recv0.at[group], s0.at[group], r0.at[group], moved("core", 1)))]

    def settle(phase, group):
        for copy in copies[phase, group]:
            copy.wait_recv()

    def reduce_first(group):
        axis = orders[group][0]
        settle(0, group)
        acc0[group] = acc0[group] + recv0[group].astype(F32)
        send1[group] = acc0[group].astype(BF16)
        copies[1, group] = []
        for step in (2, 1, 3):
            shard = (me[axis] + step) & 3
            copies[1, group].append(begin(remote(
                send1.at[group, pl.ds(shard * 16, 16)], recv1.at[group, step - 1],
                s1.at[group, step - 1], r1.at[group, step - 1], moved(axis, step),
            )))

    def reduce_second(group):
        first, axis = orders[group]
        settle(1, group)
        total = acc0[group, pl.ds(me[first] * 16, 16)]
        for step in range(3):
            total = total + recv1[group, step].astype(F32)
        acc1[group] = total
        send2[group] = total.astype(BF16)
        copies[2, group] = []
        for step in (2, 1, 3):
            shard = (me[axis] + step) & 3
            copies[2, group].append(begin(remote(
                send2.at[group, pl.ds(shard * 4, 4)], recv2.at[group, step - 1],
                s2.at[group, step - 1], r2.at[group, step - 1], moved(axis, step),
            )))

    def reduce_third(pair):
        for at in range(2):
            group = 2 * pair + at
            axis = orders[group][1]
            settle(2, group)
            total = acc1[group, pl.ds(me[axis] * 4, 4)]
            for step in range(3):
                total = total + recv2[group, step].astype(F32)
            acc2[pair, at * 4 : at * 4 + 4] = total
            send3[pair, at * 4 : at * 4 + 4] = total.astype(BF16)
        copies[3, pair] = []
        for step in (4, 3, 5, 2, 6, 1, 7):
            shard = (me["z"] + step) & 7
            copies[3, pair].append(begin(remote(
                send3.at[pair, shard], recv3.at[pair, step - 1],
                s3.at[pair, step - 1], r3.at[pair, step - 1], moved("z", step),
            )))

    def spread_third(pair):
        settle(3, pair)
        total = acc2[pair, me["z"]]
        for step in range(7):
            total = total + recv3[pair, step].astype(F32)
        own = full3.at[pair, me["z"]]
        own[...] = (total * factor).astype(BF16)
        for step in (4, 3, 5, 2, 6, 1, 7):
            begin(remote(own, own, s4.at[pair, step - 1], r4.at[pair, step - 1], moved("z", step)))

    def sender(axis, step):
        return (me[axis] + RING[axis] - step) & (RING[axis] - 1)

    def spread_second(pair):
        for step in (1, 7, 2, 6, 3, 5, 4):
            block = full3.at[pair, sender("z", step)]
            remote(block, block, s4.at[pair, step - 1], r4.at[pair, step - 1], moved("z", step)).wait_recv()
        for at in range(2):
            group = 2 * pair + at
            first, axis = orders[group]
            own = pl.ds(me[first] * 16 + me[axis] * 4, 4)
            full1[group, own] = full3[pair, at * 4 : at * 4 + 4]
            block = full1.at[group, own]
            for step in (2, 1, 3):
                begin(remote(block, block, s5.at[group, step - 1], r5.at[group, step - 1], moved(axis, step)))

    def spread_first(group):
        first, axis = orders[group]
        for step in range(1, 4):
            block = full1.at[group, pl.ds(me[first] * 16 + sender(axis, step) * 4, 4)]
            remote(block, block, s5.at[group, step - 1], r5.at[group, step - 1], moved(axis, step)).wait_recv()
        block = full1.at[group, pl.ds(me[first] * 16, 16)]
        for step in (2, 1, 3):
            begin(remote(block, block, s6.at[group, step - 1], r6.at[group, step - 1], moved(first, step)))
        to_pair(group, me[first], 0)

    def to_pair(group, shard, step):
        rows = pl.ds(shard * 16, 16)
        begin(remote(
            full1.at[group, rows], grads_ref.at[group, me["core"], rows], s7.at[group, step], r7.at[group, step], moved("core", 1)
        ))

    def spread_pair(group):
        axis = orders[group][0]
        for step in (1, 3, 2):
            block = full1.at[group, pl.ds(sender(axis, step) * 16, 16)]
            remote(block, block, s6.at[group, step - 1], r6.at[group, step - 1], moved(axis, step)).wait_recv()
            to_pair(group, sender(axis, step), step)
        keep = pltpu.make_async_copy(full1.at[group], grads_ref.at[group, me["core"]], local_s.at[8 + group])
        keep.start()
        locals_out.append(keep)

    def finish_pair(group):
        axis = orders[group][0]
        for step in range(4):
            rows = pl.ds(sender(axis, step) * 16, 16)
            remote(
                full1.at[group, rows], grads_ref.at[group, 1 - me["core"], rows], s7.at[group, step], r7.at[group, step], moved("core", 1)
            ).wait_recv()

    def give_back(at, values):
        back[at] = dot(scatter_ref[...], values).astype(BF16)
        arrived[at, 0, 0:48] = back[at, LR : LR + 48]
        arrived[at, 0, 48:128] = back[at, S1L : S1L + 80]
        arrived[at, 1, 128:288] = back[at, S2U : S2U + 160]
        routes = (
            (back.at[at, pl.ds(UR, 128)], arrived.at[at, 1, pl.ds(0, 128)], grid_moved(-1, 0)),
            (back.at[at, pl.ds(S2L, 160)], arrived.at[at, 0, pl.ds(128, 160)], grid_moved(1, 0)),
            (back.at[at, pl.ds(LL, 48)], arrived.at[at, 0, pl.ds(288, 48)], grid_moved(0, -1)),
            (back.at[at, pl.ds(UL, 48)], arrived.at[at, 1, pl.ds(288, 48)], grid_moved(-1, -1)),
        )
        return [
            begin(remote(src, dst, back_s.at[at, n], back_r.at[at, n], target))
            for n, (src, dst, target) in enumerate(routes)
        ]

    def take_back(at, arriving, out):
        for copy in arriving:
            copy.wait_recv()
        for half in range(2):
            rows = dot(unpack_ref[...], arrived[at, half]).astype(BF16)
            out_s[at, :, 3 * half : 3 * half + 3] = rows.reshape(LEVELS, 3, LONS, D)
        keep = pltpu.make_async_copy(out_s.at[at], out, local_s.at[12 + at])
        keep.start()
        locals_out.append(keep)

    def gain_copy(src, dst, sem, axis, step):
        return remote(src, dst, sg.at[sem], rg.at[sem], moved(axis, step))

    def gain_send(axis, buffer, value, first):
        own = buffer.at[me[axis]]
        own[...] = value
        for step in range(1, RING[axis]):
            begin(gain_copy(own, own, first + step, axis, step))

    def gain_take(axis, buffer, first):
        for step in range(1, RING[axis]):
            block = buffer.at[sender(axis, step)]
            gain_copy(block, block, first + step, axis, step).wait_recv()
        total = buffer[0]
        for at in range(1, RING[axis]):
            total = total + buffer[at]
        return total

    def backward(pair):
        for slot in range(4):
            rows = rows_of(slot)
            probs = probs_s[slot * 4 + pair]
            gm = gmix[rows, columns_of(0, pair)]
            grows[rows, columns_of(2, pair)] = unstack(dot(probs, gm)).astype(BF16)
            gprobs = dot_nt(stack(qkv[rows, columns_of(2, pair)]), gm).reshape(2, SPAN, SPAN)
            wide = probs.astype(F32).reshape(2, SPAN, SPAN)
            total = jnp.sum(wide * gprobs, 1, keepdims=True)
            gscores = (wide * (gprobs - total)).astype(BF16).reshape(2 * SPAN, SPAN)
            grows[rows, columns_of(0, pair)] = (dot_tn(gscores, stack(qkv[rows, columns_of(1, pair)])) * 0.125).astype(BF16)
            grows[rows, columns_of(1, pair)] = (unstack(dot(gscores, qkv[rows, columns_of(0, pair)])) * 0.125).astype(BF16)

    backward(0)
    reduce_pair(0)
    proj = dot(mixed[...], wout_ref[...]).astype(BF16)
    loads["scatter"].wait()
    lay_copies = give_back(0, (tokw[...].astype(F32) + proj.astype(F32)).astype(BF16))
    backward(1)
    reduce_pair(1)
    reduce_first(0)
    backward(2)
    reduce_pair(2)
    reduce_first(1)
    backward(3)
    reduce_pair(3)
    reduce_first(2)
    gnormed = dot_nt(grows[...], wqkv_ref[...]).astype(BF16).astype(F32)
    reduce_first(3)
    reduce_second(0)
    xhat = xhat_s[...]
    gain_rows = jnp.sum(gnormed * xhat, 0, keepdims=True)
    gain_own[...] = jnp.concatenate(
        [gain_rows[:, n * 128 : (n + 1) * 128] for n in range(4)] + [jnp.zeros((4, 128), F32)], 0
    )
    begin(gain_copy(gain_own, gain_core, 0, "core", 1))
    scaled = gnormed * gain_ref[...]
    gtok = cotw[...].astype(F32) + inv_s[...] * (
        scaled - jnp.mean(scaled, -1, keepdims=True) - xhat * jnp.mean(scaled * xhat, -1, keepdims=True)
    )
    reduce_second(1)
    gain_copy(gain_own, gain_core, 0, "core", 1).wait_recv()
    gain_send("x", gain_x, gain_own[...] + gain_core[...], 0)
    reduce_second(2)
    reduce_third(0)
    reduce_second(3)
    gain_send("y", gain_y, gain_take("x", gain_x, 0), 3)
    loads["unpack"].wait()
    take_back(0, lay_copies, lay_ref)
    reduce_third(1)
    gtok_copies = give_back(1, gtok.astype(BF16))
    spread_third(0)
    gain_send("z", gain_z, gain_take("y", gain_y, 3), 6)
    spread_third(1)
    spread_second(0)
    spread_second(1)
    spread_first(0)
    spread_first(1)
    spread_first(2)
    spread_first(3)
    take_back(1, gtok_copies, gtok_ref)
    ggain_ref[...] = gain_take("z", gain_z, 6) * factor
    spread_pair(0)
    spread_pair(1)
    spread_pair(2)
    spread_pair(3)
    for group in range(4):
        finish_pair(group)
    for copy in locals_out:
        copy.wait()
    for copy in pending:
        copy.wait_send()


def unpack_kernel(lay_in, gtok_in, grads_in, gain_in, lay_out, gtok_out, gqkv_out, gout_out, gain_out, narrow, wide, last, grids, sems):
    moves = [pltpu.make_async_copy(grads_in.at[group], narrow.at[group], sems.at[group]) for group in range(4)]
    moves += [pltpu.make_async_copy(source, grids.at[at], sems.at[4 + at]) for at, source in enumerate((lay_in, gtok_in))]
    outs = []
    for at in (4, 5, 0, 1, 2, 3):
        moves[at].start()
    for n in range(4):
        gain_out[:, n * 128 : (n + 1) * 128] = gain_in[n : n + 1]
    for at, target in enumerate((lay_out, gtok_out)):
        moves[4 + at].wait()
        outs.append(pltpu.make_async_copy(grids.at[at], target, sems.at[10 + at]))
        outs[-1].start()
    for group in range(4):
        moves[group].wait()
        for part in range(3):
            tiles = narrow[group, part // 2, (part % 2) * 32 : (part % 2 + 1) * 32]
            columns = pl.ds(part * D + group * 128, 128)
            wide[:, columns] = tiles.astype(F32).reshape(D, 128)
            outs.append(pltpu.make_async_copy(wide.at[:, columns], gqkv_out.at[:, columns], sems.at[12 + group * 3 + part]))
            outs[-1].start()
        for n in range(4):
            tiles = narrow[group, 1, 32 + n * 8 : 32 + (n + 1) * 8]
            last[group * 128 : (group + 1) * 128, n * 128 : (n + 1) * 128] = tiles.astype(F32).reshape(128, 128)
        rows = pl.ds(group * 128, 128)
        outs.append(pltpu.make_async_copy(last.at[rows], gout_out.at[rows], sems.at[6 + group]))
        outs[-1].start()
    for copy in outs:
        copy.wait()


def on_device(tokens, cotangent, norm_gain, qkv_weight, out_weight):
    pack = packing()
    tables = [jnp.asarray(table, BF16) for table in (pack, pack.T, gathering(), scattering())]
    vmem = pl.BlockSpec(memory_space=pltpu.VMEM)
    anywhere = pl.BlockSpec(memory_space=pl.ANY)
    dma = pltpu.SemaphoreType.DMA
    rows = 4 * SPAN
    scratch = [
        pltpu.VMEM(tokens.shape, BF16),
        pltpu.VMEM(tokens.shape, BF16),
        pltpu.VMEM((D, 3 * D), BF16),
        pltpu.VMEM((D, D), BF16),
        *[pltpu.VMEM(table.shape, BF16) for table in tables],
        pltpu.VMEM((2, *tokens.shape), BF16),
        pltpu.VMEM((2, 2, PACKED, D), BF16),
        pltpu.VMEM((2, STAGED, D), BF16),
        pltpu.VMEM((2, STAGED, D), BF16),
        pltpu.VMEM((2, 2, PACKED, D), BF16),
        pltpu.VMEM((rows, D), F32),
        pltpu.VMEM((rows, 1), F32),
        pltpu.VMEM((rows, D), BF16),
        pltpu.VMEM((rows, D), BF16),
        pltpu.VMEM((rows, D), BF16),
        pltpu.VMEM((rows, 3 * D), BF16),
        pltpu.VMEM((rows, D), BF16),
        pltpu.VMEM((16, 2 * SPAN, SPAN), BF16),
        pltpu.VMEM((rows, D), BF16),
        pltpu.VMEM((rows, 3 * D), BF16),
        pltpu.VMEM((4, 64, 16, 128), BF16),
        pltpu.VMEM((4, 64, 16, 128), BF16),
        pltpu.VMEM((4, 64, 16, 128), F32),
        pltpu.VMEM((4, 64, 16, 128), BF16),
        pltpu.VMEM((4, 3, 16, 16, 128), BF16),
        pltpu.VMEM((4, 16, 16, 128), F32),
        pltpu.VMEM((4, 16, 16, 128), BF16),
        pltpu.VMEM((4, 3, 4, 16, 128), BF16),
        pltpu.VMEM((2, 8, 16, 128), F32),
        pltpu.VMEM((2, 8, 16, 128), BF16),
        pltpu.VMEM((2, 7, 16, 128), BF16),
        pltpu.VMEM((2, 8, 16, 128), BF16),
        pltpu.VMEM((4, 64, 16, 128), BF16),
        pltpu.VMEM((8, 128), F32),
        pltpu.VMEM((8, 128), F32),
        pltpu.VMEM((4, 8, 128), F32),
        pltpu.VMEM((4, 8, 128), F32),
        pltpu.VMEM((8, 8, 128), F32),
        dma((14,)),
        dma((2, 6)), dma((2, 6)), dma((2, 4)), dma((2, 4)),
        dma((4,)), dma((4,)),
        dma((4, 3)), dma((4, 3)),
        dma((4, 3)), dma((4, 3)),
        dma((2, 7)), dma((2, 7)),
        dma((2, 7)), dma((2, 7)),
        dma((4, 3)), dma((4, 3)),
        dma((4, 3)), dma((4, 3)),
        dma((4, 4)), dma((4, 4)),
        dma((14,)), dma((14,)),
    ]
    grid = jax.ShapeDtypeStruct(tokens.shape, BF16)
    parts = pl.pallas_call(
        kernel,
        out_shape=(
            grid,
            grid,
            jax.ShapeDtypeStruct((4, 2, 64, 16, 128), BF16),
            jax.ShapeDtypeStruct((8, 128), F32),
        ),
        in_specs=[anywhere, anywhere, vmem] + [anywhere] * 6,
        out_specs=(anywhere, anywhere, anywhere, vmem),
        scratch_shapes=scratch,
        compiler_params=pltpu.CompilerParams(
            collective_id=0, has_side_effects=True, vmem_limit_bytes=56 * 1024 * 1024
        ),
        name="sublayer",
    )(tokens, cotangent, norm_gain.reshape(1, D), qkv_weight, out_weight, *tables)
    layer_out, grad_tokens, grad_qkv, grad_out, grad_gain = pl.pallas_call(
        unpack_kernel,
        out_shape=(
            grid,
            grid,
            jax.ShapeDtypeStruct((D, 3 * D), F32),
            jax.ShapeDtypeStruct((D, D), F32),
            jax.ShapeDtypeStruct((1, D), F32),
        ),
        in_specs=[anywhere] * 3 + [vmem],
        out_specs=(anywhere,) * 4 + (vmem,),
        scratch_shapes=[pltpu.VMEM((4, 2, 64, 16, 128), BF16), pltpu.VMEM((D, 3 * D), F32), pltpu.VMEM((D, D), F32), pltpu.VMEM((2, *tokens.shape), BF16), dma((24,))],
        compiler_params=pltpu.CompilerParams(vmem_limit_bytes=60 * 1024 * 1024),
        name="results",
    )(*parts)
    return layer_out, grad_tokens, grad_qkv, grad_out, grad_gain.reshape(D)


def solution(mesh):
    grid = P(None, "lat", "lon", None)
    return jax.shard_map(
        on_device,
        mesh=mesh,
        in_specs=(grid, grid, P(), P(), P()),
        out_specs=(grid, grid, P(), P(), P()),
        check_vma=False,
    )
```

```python
import jax
import jax.numpy as jnp
import numpy as np
from jax import lax
from jax.experimental import pallas as pl
from jax.experimental.pallas import tpu as pltpu
from jax.sharding import PartitionSpec as P

MESH = pl.DeviceIdType.MESH
F32 = jnp.float32
BF16 = jnp.bfloat16
EPSILON = 1e-05
D = 512
SPAN = 144
HALF = 72
LEVELS, LATS, LONS = 2, 6, 48
RING = {"x": 4, "y": 4, "z": 8}

RUNS = ((0, 6, 0), (6, 12, 48), (18, 12, 128), (30, 12, 208), (42, 6, 288))
PACKED = 336
UL, LL, LR, UR, S1U, S1L, S2U, S3U, S2L, S3L = 0, 48, 96, 144, 192, 272, 352, 432, 512, 592
STAGED = 672
BASES = (0, 192, 336, 416)


def packing():
    table = np.zeros((PACKED, LEVELS * 3 * LONS), np.float32)
    for first, width, row in RUNS:
        for level in range(LEVELS):
            for lat in range(3):
                for lon in range(width):
                    table[row, (level * 3 + lat) * LONS + first + lon] = 1
                    row += 1
    return table


def gathering():
    table = np.zeros((4, SPAN, 256), np.float32)
    quarter = LEVELS * 3 * 6
    for at, start in enumerate((UL, UR, LL, LR)):
        for row in range(quarter):
            table[0, at * quarter + row, start + row] = 1
    for slot, starts in ((1, (S1U, S1L)), (2, (S2U, S2L)), (3, (S3U, S3L))):
        for at, start in enumerate(starts):
            for row in range(HALF):
                table[slot, at * HALF + row, start - BASES[slot] + row] = 1
    return table


def scattering():
    gather = gathering()
    table = np.zeros((STAGED, 4 * SPAN), np.float32)
    for slot in range(4):
        table[BASES[slot] : BASES[slot] + 256, slot * SPAN : (slot + 1) * SPAN] += gather[slot].T
    return table


def dot(a, b):
    return jnp.dot(a, b, preferred_element_type=F32)


def dot_nt(a, b):
    return lax.dot_general(a, b, (((1,), (1,)), ((), ())), preferred_element_type=F32)


def dot_tn(a, b):
    return lax.dot_general(a, b, (((0,), (0,)), ((), ())), preferred_element_type=F32)


def place():
    lat, lon = lax.axis_index("lat"), lax.axis_index("lon")
    return {"x": (lon >> 1) + 2 * ((lat >> 3) & 1), "y": lat >> 4, "z": lat & 7, "core": lon & 1}


def device(at):
    return {"lat": at["y"] * 16 + (at["x"] >> 1) * 8 + at["z"], "lon": (at["x"] & 1) * 2 + at["core"]}


def targets():
    found = {("core", 1): device(dict(place(), core=1 - place()["core"]))}
    for axis, size in RING.items():
        for step in range(1, size):
            at = place()
            at[axis] = (at[axis] + step) & (size - 1)
            found[axis, step] = device(at)
    lat, lon = lax.axis_index("lat"), lax.axis_index("lon")
    for steps in ((1, 0), (-1, 0), (0, 1), (0, -1), (1, 1), (-1, -1)):
        found[steps] = {"lat": (lat + steps[0]) & 63, "lon": (lon + steps[1]) & 3}
    return found


def kernel(
    tok_hbm, cot_hbm, gain_ref, wqkv_hbm, wout_hbm, pack_hbm, unpack_hbm, gather_hbm, scatter_hbm,
    lay_ref, gtok_ref, grads_ref, ggain_ref,
    tok_ref, cot_ref, wqkv_ref, wout_ref, pack_ref, unpack_ref, gather_ref, scatter_ref, out_s,
    packed, staged, back, arrived, xhat_s, inv_s, tokw, normed, cotw, qkv, gmix, probs_s, mixed, grows,
    send0, recv0, acc0, send1, recv1, acc1, send2, recv2, acc2, send3, recv3, full3, full1,
    gain_own, gain_core, gain_x, gain_y, gain_z,
    local_s, halo_s, halo_r, back_s, back_r,
    s0, r0, s1, r1, s2, r2, s3, r3, s4, r4, s5, r5, s6, r6, s7, r7, sg, rg,
):
    pending = []
    locals_out = []

    def remote(src, dst, send_sem, recv_sem, target):
        return pltpu.make_async_remote_copy(
            src_ref=src, dst_ref=dst, send_sem=send_sem, recv_sem=recv_sem, device_id=target, device_id_type=MESH
        )

    def begin(copy):
        copy.start()
        pending.append(copy)
        return copy

    barrier = pltpu.get_barrier_semaphore()
    known = targets()
    friends = list(known.values())

    def moved(axis, step):
        return known[axis, step]

    grid_moved = moved
    loads = {}
    for at, (name, src, dst) in enumerate((
        ("tok", tok_hbm, tok_ref), ("pack", pack_hbm, pack_ref), ("cot", cot_hbm, cot_ref), ("gather", gather_hbm, gather_ref),
        ("wqkv", wqkv_hbm, wqkv_ref), ("wout", wout_hbm, wout_ref), ("scatter", scatter_hbm, scatter_ref), ("unpack", unpack_hbm, unpack_ref),
    )):
        loads[name] = pltpu.make_async_copy(src, dst, local_s.at[at])
        if at < 2:
            loads[name].start()
    for friend in friends:
        pl.semaphore_signal(barrier, inc=1, device_id=friend, device_id_type=MESH)
    for name in ("cot", "gather", "wqkv", "wout", "scatter", "unpack"):
        loads[name].start()

    me = place()
    lat = lax.axis_index("lat")

    def prepare(at, source):
        for half in range(2):
            rows = source[:, 3 * half : 3 * half + 3].reshape(LEVELS * 3 * LONS, D)
            packed[at, half] = dot(pack_ref[...], rows).astype(BF16)
        staged[at, LR : LR + 48] = packed[at, 0, 0:48]
        staged[at, S1L : S1L + 80] = packed[at, 0, 48:128]
        staged[at, S2U : S2U + 160] = packed[at, 1, 128:288]

    def halo(at):
        routes = (
            (packed.at[at, 1, pl.ds(48, 80)], staged.at[at, pl.ds(S1U, 80)], grid_moved(1, 0)),
            (packed.at[at, 0, pl.ds(128, 80)], staged.at[at, pl.ds(S2L, 80)], grid_moved(-1, 0)),
            (packed.at[at, 1, pl.ds(0, 48)], staged.at[at, pl.ds(UR, 48)], grid_moved(1, 0)),
            (packed.at[at, 0, pl.ds(208, 80)], staged.at[at, pl.ds(S3L, 80)], grid_moved(-1, 0)),
            (packed.at[at, 0, pl.ds(288, 48)], staged.at[at, pl.ds(LL, 48)], grid_moved(0, 1)),
            (packed.at[at, 1, pl.ds(288, 48)], staged.at[at, pl.ds(UL, 48)], grid_moved(1, 1)),
        )
        return [
            begin(remote(src, dst, halo_s.at[at, n], halo_r.at[at, n], target))
            for n, (src, dst, target) in enumerate(routes)
        ]

    loads["tok"].wait()
    loads["pack"].wait()
    prepare(0, tok_ref)
    pl.semaphore_wait(barrier, len(friends))
    tok_halo = halo(0)
    loads["cot"].wait()
    prepare(1, cot_ref)
    loads["gather"].wait()
    loads["wqkv"].wait()
    def enter(slot):
        rows = pl.ds(slot * SPAN, SPAN)
        x = dot(gather_ref[slot], staged[0, BASES[slot] : BASES[slot] + 256])
        tokw[rows] = x.astype(BF16)
        spread = x - jnp.mean(x, -1, keepdims=True)
        inv_std = lax.rsqrt(jnp.mean(spread * spread, -1, keepdims=True) + EPSILON)
        xhat = spread * inv_std
        xhat_s[rows] = xhat
        inv_s[rows] = inv_std
        normed[rows] = (xhat * gain_ref[...]).astype(BF16)

    def project(first, second):
        rows = jnp.concatenate([normed[slot * SPAN : (slot + 1) * SPAN] for slot in (first, second)], 0)
        for part in range(3):
            columns = pl.ds(part * D, D)
            both = dot(rows, wqkv_ref[:, columns]).astype(BF16)
            qkv[first * SPAN : (first + 1) * SPAN, columns] = both[:SPAN]
            qkv[second * SPAN : (second + 1) * SPAN, columns] = both[SPAN:]

    low_lanes = lax.broadcasted_iota(jnp.int32, (SPAN, 128), 1) < 64
    apart = (lax.broadcasted_iota(jnp.int32, (SPAN, SPAN), 0) < HALF) != (
        lax.broadcasted_iota(jnp.int32, (SPAN, SPAN), 1) < HALF
    )

    def stack(block):
        zero = jnp.zeros_like(block)
        return jnp.concatenate([jnp.where(low_lanes, block, zero), jnp.where(low_lanes, zero, block)], 0)

    def unstack(block):
        return jnp.where(low_lanes, block[:SPAN], block[SPAN:])

    def rows_of(slot):
        return pl.ds(slot * SPAN, SPAN)

    def columns_of(part, pair):
        return pl.ds(part * D + pair * 128, 128)

    def forward(slot):
        rows = rows_of(slot)
        cut = lat == (0 if slot < 2 else 63)
        bias = jnp.where(apart & cut, -1e30, 0.0)
        for pair in range(4):
            k = stack(qkv[rows, columns_of(1, pair)])
            scores = dot_nt(k, qkv[rows, columns_of(0, pair)]).reshape(2, SPAN, SPAN) + bias
            peak = jnp.max(scores, 1, keepdims=True)
            weights = jnp.exp2((scores - peak) * (0.125 * 1.4426950408889634))
            probs = weights * (1.0 / jnp.sum(weights, 1, keepdims=True))
            probs = probs.astype(BF16).reshape(2 * SPAN, SPAN)
            probs_s[slot * 4 + pair] = probs
            mixed[rows, columns_of(0, pair)] = dot_tn(probs, stack(qkv[rows, columns_of(2, pair)])).astype(BF16)

    cot_halo = halo(1)
    for copy in tok_halo[:2]:
        copy.wait_recv()
    enter(1)
    enter(2)
    project(1, 2)
    forward(1)
    forward(2)
    for copy in tok_halo[2:]:
        copy.wait_recv()
    enter(0)
    enter(3)
    project(0, 3)
    forward(0)
    forward(3)

    loads["wout"].wait()
    for copy in cot_halo:
        copy.wait_recv()
    for slot in range(4):
        rows = pl.ds(slot * SPAN, SPAN)
        cotw[rows] = dot(gather_ref[slot], staged[1, BASES[slot] : BASES[slot] + 256]).astype(BF16)
    gmix[...] = dot_nt(cotw[...], wout_ref[...]).astype(BF16)

    orders = (("x", "y"), ("y", "x"), ("x", "y"), ("y", "x"))
    factor = 1.0 / np.sqrt(np.float32(147456))
    copies = {}
    first_core = me["core"] == 0

    def reduce_pair(group):
        columns = jnp.concatenate([grows[:, part * D + group * 128 : part * D + (group + 1) * 128] for part in range(3)], 1)
        total = dot_tn(normed[...], columns)
        rows = dot_tn(mixed[:, group * 128 : (group + 1) * 128], cotw[...])
        total = [total[:, n * 128 : (n + 1) * 128].reshape(32, 16, 128) for n in range(3)]
        total.append(jnp.concatenate([rows[:, n * 128 : (n + 1) * 128].reshape(8, 16, 128) for n in range(4)], 0))
        for n in range(2):
            acc0[group, n * 32 : (n + 1) * 32] = jnp.where(first_core, total[n], total[n + 2])
            send0[group, n * 32 : (n + 1) * 32] = jnp.where(first_core, total[n + 2], total[n]).astype(BF16)
        copies[0, group] = [begin(remote(send0.at[group], recv0.at[group], s0.at[group], r0.at[group], moved("core", 1)))]

    def settle(phase, group):
        for copy in copies[phase, group]:
            copy.wait_recv()

    def reduce_first(group):
        axis = orders[group][0]
        settle(0, group)
        acc0[group] = acc0[group] + recv0[group].astype(F32)
        send1[group] = acc0[group].astype(BF16)
        copies[1, group] = []
        for step in (2, 1, 3):
            shard = (me[axis] + step) & 3
            copies[1, group].append(begin(remote(
                send1.at[group, pl.ds(shard * 16, 16)], recv1.at[group, step - 1],
                s1.at[group, step - 1], r1.at[group, step - 1], moved(axis, step),
            )))

    def reduce_second(group):
        first, axis = orders[group]
        settle(1, group)
        total = acc0[group, pl.ds(me[first] * 16, 16)]
        for step in range(3):
            total = total + recv1[group, step].astype(F32)
        acc1[group] = total
        send2[group] = total.astype(BF16)
        copies[2, group] = []
        for step in (2, 1, 3):
            shard = (me[axis] + step) & 3
            copies[2, group].append(begin(remote(
                send2.at[group, pl.ds(shard * 4, 4)], recv2.at[group, step - 1],
                s2.at[group, step - 1], r2.at[group, step - 1], moved(axis, step),
            )))

    def reduce_third(pair):
        for at in range(2):
            group = 2 * pair + at
            axis = orders[group][1]
            settle(2, group)
            total = acc1[group, pl.ds(me[axis] * 4, 4)]
            for step in range(3):
                total = total + recv2[group, step].astype(F32)
            acc2[pair, at * 4 : at * 4 + 4] = total
            send3[pair, at * 4 : at * 4 + 4] = total.astype(BF16)
        copies[3, pair] = []
        for step in (4, 3, 5, 2, 6, 1, 7):
            shard = (me["z"] + step) & 7
            copies[3, pair].append(begin(remote(
                send3.at[pair, shard], recv3.at[pair, step - 1],
                s3.at[pair, step - 1], r3.at[pair, step - 1], moved("z", step),
            )))

    def spread_third(pair):
        settle(3, pair)
        total = acc2[pair, me["z"]]
        for step in range(7):
            total = total + recv3[pair, step].astype(F32)
        own = full3.at[pair, me["z"]]
        own[...] = (total * factor).astype(BF16)
        for step in (4, 3, 5, 2, 6, 1, 7):
            begin(remote(own, own, s4.at[pair, step - 1], r4.at[pair, step - 1], moved("z", step)))

    def sender(axis, step):
        return (me[axis] + RING[axis] - step) & (RING[axis] - 1)

    def spread_second(pair):
        for step in (1, 7, 2, 6, 3, 5, 4):
            block = full3.at[pair, sender("z", step)]
            remote(block, block, s4.at[pair, step - 1], r4.at[pair, step - 1], moved("z", step)).wait_recv()
        for at in range(2):
            group = 2 * pair + at
            first, axis = orders[group]
            own = pl.ds(me[first] * 16 + me[axis] * 4, 4)
            full1[group, own] = full3[pair, at * 4 : at * 4 + 4]
            block = full1.at[group, own]
            for step in (2, 1, 3):
                begin(remote(block, block, s5.at[group, step - 1], r5.at[group, step - 1], moved(axis, step)))

    def spread_first(group):
        first, axis = orders[group]
        for step in range(1, 4):
            block = full1.at[group, pl.ds(me[first] * 16 + sender(axis, step) * 4, 4)]
            remote(block, block, s5.at[group, step - 1], r5.at[group, step - 1], moved(axis, step)).wait_recv()
        block = full1.at[group, pl.ds(me[first] * 16, 16)]
        for step in (2, 1, 3):
            begin(remote(block, block, s6.at[group, step - 1], r6.at[group, step - 1], moved(first, step)))
        to_pair(group, me[first], 0)

    def to_pair(group, shard, step):
        rows = pl.ds(shard * 16, 16)
        begin(remote(
            full1.at[group, rows], grads_ref.at[group, me["core"], rows], s7.at[group, step], r7.at[group, step], moved("core", 1)
        ))

    def spread_pair(group):
        axis = orders[group][0]
        for step in (1, 3, 2):
            block = full1.at[group, pl.ds(sender(axis, step) * 16, 16)]
            remote(block, block, s6.at[group, step - 1], r6.at[group, step - 1], moved(axis, step)).wait_recv()
            to_pair(group, sender(axis, step), step)
        keep = pltpu.make_async_copy(full1.at[group], grads_ref.at[group, me["core"]], local_s.at[8 + group])
        keep.start()
        locals_out.append(keep)

    def finish_pair(group):
        axis = orders[group][0]
        for step in range(4):
            rows = pl.ds(sender(axis, step) * 16, 16)
            remote(
                full1.at[group, rows], grads_ref.at[group, 1 - me["core"], rows], s7.at[group, step], r7.at[group, step], moved("core", 1)
            ).wait_recv()

    def give_back(at, values):
        back[at] = dot(scatter_ref[...], values).astype(BF16)
        arrived[at, 0, 0:48] = back[at, LR : LR + 48]
        arrived[at, 0, 48:128] = back[at, S1L : S1L + 80]
        arrived[at, 1, 128:288] = back[at, S2U : S2U + 160]
        routes = (
            (back.at[at, pl.ds(UR, 128)], arrived.at[at, 1, pl.ds(0, 128)], grid_moved(-1, 0)),
            (back.at[at, pl.ds(S2L, 160)], arrived.at[at, 0, pl.ds(128, 160)], grid_moved(1, 0)),
            (back.at[at, pl.ds(LL, 48)], arrived.at[at, 0, pl.ds(288, 48)], grid_moved(0, -1)),
            (back.at[at, pl.ds(UL, 48)], arrived.at[at, 1, pl.ds(288, 48)], grid_moved(-1, -1)),
        )
        return [
            begin(remote(src, dst, back_s.at[at, n], back_r.at[at, n], target))
            for n, (src, dst, target) in enumerate(routes)
        ]

    def take_back(at, arriving, out):
        for copy in arriving:
            copy.wait_recv()
        for half in range(2):
            rows = dot(unpack_ref[...], arrived[at, half]).astype(BF16)
            out_s[at, :, 3 * half : 3 * half + 3] = rows.reshape(LEVELS, 3, LONS, D)
        keep = pltpu.make_async_copy(out_s.at[at], out, local_s.at[12 + at])
        keep.start()
        locals_out.append(keep)

    def gain_copy(src, dst, sem, axis, step):
        return remote(src, dst, sg.at[sem], rg.at[sem], moved(axis, step))

    def gain_send(axis, buffer, value, first):
        own = buffer.at[me[axis]]
        own[...] = value
        for step in range(1, RING[axis]):
            begin(gain_copy(own, own, first + step, axis, step))

    def gain_take(axis, buffer, first):
        for step in range(1, RING[axis]):
            block = buffer.at[sender(axis, step)]
            gain_copy(block, block, first + step, axis, step).wait_recv()
        total = buffer[0]
        for at in range(1, RING[axis]):
            total = total + buffer[at]
        return total

    def backward(pair):
        for slot in range(4):
            rows = rows_of(slot)
            probs = probs_s[slot * 4 + pair]
            gm = gmix[rows, columns_of(0, pair)]
            grows[rows, columns_of(2, pair)] = unstack(dot(probs, gm)).astype(BF16)
            gprobs = dot_nt(stack(qkv[rows, columns_of(2, pair)]), gm).reshape(2, SPAN, SPAN)
            wide = probs.astype(F32).reshape(2, SPAN, SPAN)
            total = jnp.sum(wide * gprobs, 1, keepdims=True)
            gscores = (wide * (gprobs - total)).astype(BF16).reshape(2 * SPAN, SPAN)
            grows[rows, columns_of(0, pair)] = (dot_tn(gscores, stack(qkv[rows, columns_of(1, pair)])) * 0.125).astype(BF16)
            grows[rows, columns_of(1, pair)] = (unstack(dot(gscores, qkv[rows, columns_of(0, pair)])) * 0.125).astype(BF16)

    backward(0)
    reduce_pair(0)
    proj = dot(mixed[...], wout_ref[...]).astype(BF16)
    loads["scatter"].wait()
    lay_copies = give_back(0, (tokw[...].astype(F32) + proj.astype(F32)).astype(BF16))
    backward(1)
    reduce_pair(1)
    reduce_first(0)
    backward(2)
    reduce_pair(2)
    reduce_first(1)
    backward(3)
    reduce_pair(3)
    reduce_first(2)
    gnormed = dot_nt(grows[...], wqkv_ref[...]).astype(BF16).astype(F32)
    reduce_first(3)
    reduce_second(0)
    xhat = xhat_s[...]
    gain_rows = jnp.sum(gnormed * xhat, 0, keepdims=True)
    gain_own[...] = jnp.concatenate(
        [gain_rows[:, n * 128 : (n + 1) * 128] for n in range(4)] + [jnp.zeros((4, 128), F32)], 0
    )
    begin(gain_copy(gain_own, gain_core, 0, "core", 1))
    scaled = gnormed * gain_ref[...]
    gtok = cotw[...].astype(F32) + inv_s[...] * (
        scaled - jnp.mean(scaled, -1, keepdims=True) - xhat * jnp.mean(scaled * xhat, -1, keepdims=True)
    )
    reduce_second(1)
    gain_copy(gain_own, gain_core, 0, "core", 1).wait_recv()
    gain_send("x", gain_x, gain_own[...] + gain_core[...], 0)
    reduce_second(2)
    reduce_third(0)
    reduce_second(3)
    gain_send("y", gain_y, gain_take("x", gain_x, 0), 3)
    loads["unpack"].wait()
    take_back(0, lay_copies, lay_ref)
    reduce_third(1)
    gtok_copies = give_back(1, gtok.astype(BF16))
    spread_third(0)
    gain_send("z", gain_z, gain_take("y", gain_y, 3), 6)
    spread_third(1)
    spread_second(0)
    spread_second(1)
    spread_first(0)
    spread_first(1)
    spread_first(2)
    spread_first(3)
    take_back(1, gtok_copies, gtok_ref)
    ggain_ref[...] = gain_take("z", gain_z, 6) * factor
    spread_pair(0)
    spread_pair(1)
    spread_pair(2)
    spread_pair(3)
    for group in range(4):
        finish_pair(group)
    for copy in locals_out:
        copy.wait()
    for copy in pending:
        copy.wait_send()


def unpack_kernel(lay_in, gtok_in, grads_in, gain_in, lay_out, gtok_out, gqkv_out, gout_out, gain_out, narrow, wide, last, grids, sems):
    moves = [pltpu.make_async_copy(grads_in.at[group], narrow.at[group], sems.at[group]) for group in range(4)]
    moves += [pltpu.make_async_copy(source, grids.at[at], sems.at[4 + at]) for at, source in enumerate((lay_in, gtok_in))]
    outs = []
    for at in (4, 5, 0, 1, 2, 3):
        moves[at].start()
    for n in range(4):
        gain_out[:, n * 128 : (n + 1) * 128] = gain_in[n : n + 1]
    for at, target in enumerate((lay_out, gtok_out)):
        moves[4 + at].wait()
        outs.append(pltpu.make_async_copy(grids.at[at], target, sems.at[10 + at]))
        outs[-1].start()
    for group in range(4):
        moves[group].wait()
        for part in range(3):
            tiles = narrow[group, part // 2, (part % 2) * 32 : (part % 2 + 1) * 32]
            columns = pl.ds(part * D + group * 128, 128)
            wide[:, columns] = tiles.astype(F32).reshape(D, 128)
            outs.append(pltpu.make_async_copy(wide.at[:, columns], gqkv_out.at[:, columns], sems.at[12 + group * 3 + part]))
            outs[-1].start()
        for n in range(4):
            tiles = narrow[group, 1, 32 + n * 8 : 32 + (n + 1) * 8]
            last[group * 128 : (group + 1) * 128, n * 128 : (n + 1) * 128] = tiles.astype(F32).reshape(128, 128)
        rows = pl.ds(group * 128, 128)
        outs.append(pltpu.make_async_copy(last.at[rows], gout_out.at[rows], sems.at[6 + group]))
        outs[-1].start()
    for copy in outs:
        copy.wait()


def on_device(tokens, cotangent, norm_gain, qkv_weight, out_weight):
    pack = packing()
    tables = [jnp.asarray(table, BF16) for table in (pack, pack.T, gathering(), scattering())]
    vmem = pl.BlockSpec(memory_space=pltpu.VMEM)
    anywhere = pl.BlockSpec(memory_space=pl.ANY)
    dma = pltpu.SemaphoreType.DMA
    rows = 4 * SPAN
    scratch = [
        pltpu.VMEM(tokens.shape, BF16),
        pltpu.VMEM(tokens.shape, BF16),
        pltpu.VMEM((D, 3 * D), BF16),
        pltpu.VMEM((D, D), BF16),
        *[pltpu.VMEM(table.shape, BF16) for table in tables],
        pltpu.VMEM((2, *tokens.shape), BF16),
        pltpu.VMEM((2, 2, PACKED, D), BF16),
        pltpu.VMEM((2, STAGED, D), BF16),
        pltpu.VMEM((2, STAGED, D), BF16),
        pltpu.VMEM((2, 2, PACKED, D), BF16),
        pltpu.VMEM((rows, D), F32),
        pltpu.VMEM((rows, 1), F32),
        pltpu.VMEM((rows, D), BF16),
        pltpu.VMEM((rows, D), BF16),
        pltpu.VMEM((rows, D), BF16),
        pltpu.VMEM((rows, 3 * D), BF16),
        pltpu.VMEM((rows, D), BF16),
        pltpu.VMEM((16, 2 * SPAN, SPAN), BF16),
        pltpu.VMEM((rows, D), BF16),
        pltpu.VMEM((rows, 3 * D), BF16),
        pltpu.VMEM((4, 64, 16, 128), BF16),
        pltpu.VMEM((4, 64, 16, 128), BF16),
        pltpu.VMEM((4, 64, 16, 128), F32),
        pltpu.VMEM((4, 64, 16, 128), BF16),
        pltpu.VMEM((4, 3, 16, 16, 128), BF16),
        pltpu.VMEM((4, 16, 16, 128), F32),
        pltpu.VMEM((4, 16, 16, 128), BF16),
        pltpu.VMEM((4, 3, 4, 16, 128), BF16),
        pltpu.VMEM((2, 8, 16, 128), F32),
        pltpu.VMEM((2, 8, 16, 128), BF16),
        pltpu.VMEM((2, 7, 16, 128), BF16),
        pltpu.VMEM((2, 8, 16, 128), BF16),
        pltpu.VMEM((4, 64, 16, 128), BF16),
        pltpu.VMEM((8, 128), F32),
        pltpu.VMEM((8, 128), F32),
        pltpu.VMEM((4, 8, 128), F32),
        pltpu.VMEM((4, 8, 128), F32),
        pltpu.VMEM((8, 8, 128), F32),
        dma((14,)),
        dma((2, 6)), dma((2, 6)), dma((2, 4)), dma((2, 4)),
        dma((4,)), dma((4,)),
        dma((4, 3)), dma((4, 3)),
        dma((4, 3)), dma((4, 3)),
        dma((2, 7)), dma((2, 7)),
        dma((2, 7)), dma((2, 7)),
        dma((4, 3)), dma((4, 3)),
        dma((4, 3)), dma((4, 3)),
        dma((4, 4)), dma((4, 4)),
        dma((14,)), dma((14,)),
    ]
    grid = jax.ShapeDtypeStruct(tokens.shape, BF16)
    parts = pl.pallas_call(
        kernel,
        out_shape=(
            grid,
            grid,
            jax.ShapeDtypeStruct((4, 2, 64, 16, 128), BF16),
            jax.ShapeDtypeStruct((8, 128), F32),
        ),
        in_specs=[anywhere, anywhere, vmem] + [anywhere] * 6,
        out_specs=(anywhere, anywhere, anywhere, vmem),
        scratch_shapes=scratch,
        compiler_params=pltpu.CompilerParams(
            collective_id=0, has_side_effects=True, vmem_limit_bytes=56 * 1024 * 1024
        ),
        name="sublayer",
    )(tokens, cotangent, norm_gain.reshape(1, D), qkv_weight, out_weight, *tables)
    layer_out, grad_tokens, grad_qkv, grad_out, grad_gain = pl.pallas_call(
        unpack_kernel,
        out_shape=(
            grid,
            grid,
            jax.ShapeDtypeStruct((D, 3 * D), F32),
            jax.ShapeDtypeStruct((D, D), F32),
            jax.ShapeDtypeStruct((1, D), F32),
        ),
        in_specs=[anywhere] * 3 + [vmem],
        out_specs=(anywhere,) * 4 + (vmem,),
        scratch_shapes=[pltpu.VMEM((4, 2, 64, 16, 128), BF16), pltpu.VMEM((D, 3 * D), F32), pltpu.VMEM((D, D), F32), pltpu.VMEM((2, *tokens.shape), BF16), dma((24,))],
        compiler_params=pltpu.CompilerParams(vmem_limit_bytes=60 * 1024 * 1024),
        name="results",
    )(*parts)
    return layer_out, grad_tokens, grad_qkv, grad_out, grad_gain.reshape(D)


def solution(mesh):
    grid = P(None, "lat", "lon", None)
    return jax.shard_map(
        on_device,
        mesh=mesh,
        in_specs=(grid, grid, P(), P(), P()),
        out_specs=(grid, grid, P(), P(), P()),
        check_vma=False,
    )
```

```python
import jax
import jax.numpy as jnp
import numpy as np
from jax import lax
from jax.experimental import pallas as pl
from jax.experimental.pallas import tpu as pltpu
from jax.sharding import PartitionSpec as P

MESH = pl.DeviceIdType.MESH
F32 = jnp.float32
BF16 = jnp.bfloat16
EPSILON = 1e-05
D = 512
SPAN = 144
HALF = 72
LEVELS, LATS, LONS = 2, 6, 48
RING = {"x": 4, "y": 4, "z": 8}

RUNS = ((0, 6, 0), (6, 12, 48), (18, 12, 128), (30, 12, 208), (42, 6, 288))
PACKED = 336
UL, LL, LR, UR, S1U, S1L, S2U, S3U, S2L, S3L = 0, 48, 96, 144, 192, 272, 352, 432, 512, 592
STAGED = 672
BASES = (0, 192, 336, 416)


def packing():
    table = np.zeros((PACKED, LEVELS * 3 * LONS), np.float32)
    for first, width, row in RUNS:
        for level in range(LEVELS):
            for lat in range(3):
                for lon in range(width):
                    table[row, (level * 3 + lat) * LONS + first + lon] = 1
                    row += 1
    return table


def gathering():
    table = np.zeros((4, SPAN, 256), np.float32)
    quarter = LEVELS * 3 * 6
    for at, start in enumerate((UL, UR, LL, LR)):
        for row in range(quarter):
            table[0, at * quarter + row, start + row] = 1
    for slot, starts in ((1, (S1U, S1L)), (2, (S2U, S2L)), (3, (S3U, S3L))):
        for at, start in enumerate(starts):
            for row in range(HALF):
                table[slot, at * HALF + row, start - BASES[slot] + row] = 1
    return table


def scattering():
    gather = gathering()
    table = np.zeros((STAGED, 4 * SPAN), np.float32)
    for slot in range(4):
        table[BASES[slot] : BASES[slot] + 256, slot * SPAN : (slot + 1) * SPAN] += gather[slot].T
    return table


def dot(a, b):
    return jnp.dot(a, b, preferred_element_type=F32)


def dot_nt(a, b):
    return lax.dot_general(a, b, (((1,), (1,)), ((), ())), preferred_element_type=F32)


def dot_tn(a, b):
    return lax.dot_general(a, b, (((0,), (0,)), ((), ())), preferred_element_type=F32)


def place():
    lat, lon = lax.axis_index("lat"), lax.axis_index("lon")
    return {"x": (lon >> 1) + 2 * ((lat >> 3) & 1), "y": lat >> 4, "z": lat & 7, "core": lon & 1}


def device(at):
    return {"lat": at["y"] * 16 + (at["x"] >> 1) * 8 + at["z"], "lon": (at["x"] & 1) * 2 + at["core"]}


def targets():
    found = {("core", 1): device(dict(place(), core=1 - place()["core"]))}
    for axis, size in RING.items():
        for step in range(1, size):
            at = place()
            at[axis] = (at[axis] + step) & (size - 1)
            found[axis, step] = device(at)
    lat, lon = lax.axis_index("lat"), lax.axis_index("lon")
    for steps in ((1, 0), (-1, 0), (0, 1), (0, -1), (1, 1), (-1, -1)):
        found[steps] = {"lat": (lat + steps[0]) & 63, "lon": (lon + steps[1]) & 3}
    return found


def kernel(
    tok_hbm, cot_hbm, gain_ref, wqkv_hbm, wout_hbm, pack_hbm, unpack_hbm, gather_hbm, scatter_hbm,
    lay_ref, gtok_ref, grads_ref, ggain_ref,
    tok_ref, cot_ref, wqkv_ref, wout_ref, pack_ref, unpack_ref, gather_ref, scatter_ref, out_s,
    packed, staged, back, arrived, xhat_s, inv_s, tokw, normed, cotw, qkv, gmix, probs_s, mixed, grows,
    send0, recv0, acc0, send1, recv1, acc1, send2, recv2, acc2, send3, recv3, full3, full1,
    gain_own, gain_core, gain_x, gain_y, gain_z,
    local_s, halo_s, halo_r, back_s, back_r,
    s0, r0, s1, r1, s2, r2, s3, r3, s4, r4, s5, r5, s6, r6, s7, r7, sg, rg,
):
    pending = []
    locals_out = []

    def remote(src, dst, send_sem, recv_sem, target):
        return pltpu.make_async_remote_copy(
            src_ref=src, dst_ref=dst, send_sem=send_sem, recv_sem=recv_sem, device_id=target, device_id_type=MESH
        )

    def begin(copy):
        copy.start()
        pending.append(copy)
        return copy

    barrier = pltpu.get_barrier_semaphore()
    known = targets()
    friends = list(known.values())

    def moved(axis, step):
        return known[axis, step]

    grid_moved = moved
    loads = {}
    for at, (name, src, dst) in enumerate((
        ("tok", tok_hbm, tok_ref), ("pack", pack_hbm, pack_ref), ("cot", cot_hbm, cot_ref), ("gather", gather_hbm, gather_ref),
        ("wqkv", wqkv_hbm, wqkv_ref), ("wout", wout_hbm, wout_ref), ("scatter", scatter_hbm, scatter_ref), ("unpack", unpack_hbm, unpack_ref),
    )):
        loads[name] = pltpu.make_async_copy(src, dst, local_s.at[at])
        if at < 2:
            loads[name].start()
    for friend in friends:
        pl.semaphore_signal(barrier, inc=1, device_id=friend, device_id_type=MESH)
    for name in ("cot", "gather", "wqkv", "wout", "scatter", "unpack"):
        loads[name].start()

    me = place()
    lat = lax.axis_index("lat")

    def prepare(at, source):
        for half in range(2):
            rows = source[:, 3 * half : 3 * half + 3].reshape(LEVELS * 3 * LONS, D)
            packed[at, half] = dot(pack_ref[...], rows).astype(BF16)
        staged[at, LR : LR + 48] = packed[at, 0, 0:48]
        staged[at, S1L : S1L + 80] = packed[at, 0, 48:128]
        staged[at, S2U : S2U + 160] = packed[at, 1, 128:288]

    def halo(at):
        routes = (
            (packed.at[at, 1, pl.ds(48, 80)], staged.at[at, pl.ds(S1U, 80)], grid_moved(1, 0)),
            (packed.at[at, 0, pl.ds(128, 80)], staged.at[at, pl.ds(S2L, 80)], grid_moved(-1, 0)),
            (packed.at[at, 1, pl.ds(0, 48)], staged.at[at, pl.ds(UR, 48)], grid_moved(1, 0)),
            (packed.at[at, 0, pl.ds(208, 80)], staged.at[at, pl.ds(S3L, 80)], grid_moved(-1, 0)),
            (packed.at[at, 0, pl.ds(288, 48)], staged.at[at, pl.ds(LL, 48)], grid_moved(0, 1)),
            (packed.at[at, 1, pl.ds(288, 48)], staged.at[at, pl.ds(UL, 48)], grid_moved(1, 1)),
        )
        return [
            begin(remote(src, dst, halo_s.at[at, n], halo_r.at[at, n], target))
            for n, (src, dst, target) in enumerate(routes)
        ]

    loads["tok"].wait()
    loads["pack"].wait()
    prepare(0, tok_ref)
    pl.semaphore_wait(barrier, len(friends))
    tok_halo = halo(0)
    loads["cot"].wait()
    prepare(1, cot_ref)
    loads["gather"].wait()
    loads["wqkv"].wait()
    def enter(slot):
        rows = pl.ds(slot * SPAN, SPAN)
        x = dot(gather_ref[slot], staged[0, BASES[slot] : BASES[slot] + 256])
        tokw[rows] = x.astype(BF16)
        spread = x - jnp.mean(x, -1, keepdims=True)
        inv_std = lax.rsqrt(jnp.mean(spread * spread, -1, keepdims=True) + EPSILON)
        xhat = spread * inv_std
        xhat_s[rows] = xhat
        inv_s[rows] = inv_std
        normed[rows] = (xhat * gain_ref[...]).astype(BF16)

    def project(first, second):
        rows = jnp.concatenate([normed[slot * SPAN : (slot + 1) * SPAN] for slot in (first, second)], 0)
        for part in range(3):
            columns = pl.ds(part * D, D)
            both = dot(rows, wqkv_ref[:, columns]).astype(BF16)
            qkv[first * SPAN : (first + 1) * SPAN, columns] = both[:SPAN]
            qkv[second * SPAN : (second + 1) * SPAN, columns] = both[SPAN:]

    low_lanes = lax.broadcasted_iota(jnp.int32, (SPAN, 128), 1) < 64
    apart = (lax.broadcasted_iota(jnp.int32, (SPAN, SPAN), 0) < HALF) != (
        lax.broadcasted_iota(jnp.int32, (SPAN, SPAN), 1) < HALF
    )

    def stack(block):
        zero = jnp.zeros_like(block)
        return jnp.concatenate([jnp.where(low_lanes, block, zero), jnp.where(low_lanes, zero, block)], 0)

    def unstack(block):
        return jnp.where(low_lanes, block[:SPAN], block[SPAN:])

    def rows_of(slot):
        return pl.ds(slot * SPAN, SPAN)

    def columns_of(part, pair):
        return pl.ds(part * D + pair * 128, 128)

    def forward(slot):
        rows = rows_of(slot)
        cut = lat == (0 if slot < 2 else 63)
        bias = jnp.where(apart & cut, -1e30, 0.0)
        for pair in range(4):
            k = stack(qkv[rows, columns_of(1, pair)])
            scores = dot_nt(k, qkv[rows, columns_of(0, pair)]).reshape(2, SPAN, SPAN) + bias
            peak = jnp.max(scores, 1, keepdims=True)
            weights = jnp.exp2((scores - peak) * (0.125 * 1.4426950408889634))
            probs = weights * (1.0 / jnp.sum(weights, 1, keepdims=True))
            probs = probs.astype(BF16).reshape(2 * SPAN, SPAN)
            probs_s[slot * 4 + pair] = probs
            mixed[rows, columns_of(0, pair)] = dot_tn(probs, stack(qkv[rows, columns_of(2, pair)])).astype(BF16)

    cot_halo = halo(1)
    for copy in tok_halo[:2]:
        copy.wait_recv()
    enter(1)
    enter(2)
    project(1, 2)
    forward(1)
    forward(2)
    for copy in tok_halo[2:]:
        copy.wait_recv()
    enter(0)
    enter(3)
    project(0, 3)
    forward(0)
    forward(3)

    loads["wout"].wait()
    for copy in cot_halo:
        copy.wait_recv()
    for slot in range(4):
        rows = pl.ds(slot * SPAN, SPAN)
        cotw[rows] = dot(gather_ref[slot], staged[1, BASES[slot] : BASES[slot] + 256]).astype(BF16)
    gmix[...] = dot_nt(cotw[...], wout_ref[...]).astype(BF16)

    orders = (("x", "y"), ("y", "x"), ("x", "y"), ("y", "x"))
    factor = 1.0 / np.sqrt(np.float32(147456))
    copies = {}
    first_core = me["core"] == 0

    def reduce_pair(group):
        columns = jnp.concatenate([grows[:, part * D + group * 128 : part * D + (group + 1) * 128] for part in range(3)], 1)
        total = dot_tn(normed[...], columns)
        rows = dot_tn(mixed[:, group * 128 : (group + 1) * 128], cotw[...])
        total = [total[:, n * 128 : (n + 1) * 128].reshape(32, 16, 128) for n in range(3)]
        total.append(jnp.concatenate([rows[:, n * 128 : (n + 1) * 128].reshape(8, 16, 128) for n in range(4)], 0))
        for n in range(2):
            acc0[group, n * 32 : (n + 1) * 32] = jnp.where(first_core, total[n], total[n + 2])
            send0[group, n * 32 : (n + 1) * 32] = jnp.where(first_core, total[n + 2], total[n]).astype(BF16)
        copies[0, group] = [begin(remote(send0.at[group], recv0.at[group], s0.at[group], r0.at[group], moved("core", 1)))]

    def settle(phase, group):
        for copy in copies[phase, group]:
            copy.wait_recv()

    def reduce_first(group):
        axis = orders[group][0]
        settle(0, group)
        acc0[group] = acc0[group] + recv0[group].astype(F32)
        send1[group] = acc0[group].astype(BF16)
        copies[1, group] = []
        for step in (2, 1, 3):
            shard = (me[axis] + step) & 3
            copies[1, group].append(begin(remote(
                send1.at[group, pl.ds(shard * 16, 16)], recv1.at[group, step - 1],
                s1.at[group, step - 1], r1.at[group, step - 1], moved(axis, step),
            )))

    def reduce_second(group):
        first, axis = orders[group]
        settle(1, group)
        total = acc0[group, pl.ds(me[first] * 16, 16)]
        for step in range(3):
            total = total + recv1[group, step].astype(F32)
        acc1[group] = total
        send2[group] = total.astype(BF16)
        copies[2, group] = []
        for step in (2, 1, 3):
            shard = (me[axis] + step) & 3
            copies[2, group].append(begin(remote(
                send2.at[group, pl.ds(shard * 4, 4)], recv2.at[group, step - 1],
                s2.at[group, step - 1], r2.at[group, step - 1], moved(axis, step),
            )))

    def reduce_third(pair):
        for at in range(2):
            group = 2 * pair + at
            axis = orders[group][1]
            settle(2, group)
            total = acc1[group, pl.ds(me[axis] * 4, 4)]
            for step in range(3):
                total = total + recv2[group, step].astype(F32)
            acc2[pair, at * 4 : at * 4 + 4] = total
            send3[pair, at * 4 : at * 4 + 4] = total.astype(BF16)
        copies[3, pair] = []
        for step in (4, 3, 5, 2, 6, 1, 7):
            shard = (me["z"] + step) & 7
            copies[3, pair].append(begin(remote(
                send3.at[pair, shard], recv3.at[pair, step - 1],
                s3.at[pair, step - 1], r3.at[pair, step - 1], moved("z", step),
            )))

    def spread_third(pair):
        settle(3, pair)
        total = acc2[pair, me["z"]]
        for step in range(7):
            total = total + recv3[pair, step].astype(F32)
        own = full3.at[pair, me["z"]]
        own[...] = (total * factor).astype(BF16)
        for step in (4, 3, 5, 2, 6, 1, 7):
            begin(remote(own, own, s4.at[pair, step - 1], r4.at[pair, step - 1], moved("z", step)))

    def sender(axis, step):
        return (me[axis] + RING[axis] - step) & (RING[axis] - 1)

    def spread_second(pair):
        for step in (1, 7, 2, 6, 3, 5, 4):
            block = full3.at[pair, sender("z", step)]
            remote(block, block, s4.at[pair, step - 1], r4.at[pair, step - 1], moved("z", step)).wait_recv()
        for at in range(2):
            group = 2 * pair + at
            first, axis = orders[group]
            own = pl.ds(me[first] * 16 + me[axis] * 4, 4)
            full1[group, own] = full3[pair, at * 4 : at * 4 + 4]
            block = full1.at[group, own]
            for step in (2, 1, 3):
                begin(remote(block, block, s5.at[group, step - 1], r5.at[group, step - 1], moved(axis, step)))

    def spread_first(group):
        first, axis = orders[group]
        for step in range(1, 4):
            block = full1.at[group, pl.ds(me[first] * 16 + sender(axis, step) * 4, 4)]
            remote(block, block, s5.at[group, step - 1], r5.at[group, step - 1], moved(axis, step)).wait_recv()
        block = full1.at[group, pl.ds(me[first] * 16, 16)]
        for step in (2, 1, 3):
            begin(remote(block, block, s6.at[group, step - 1], r6.at[group, step - 1], moved(first, step)))
        to_pair(group, me[first], 0)

    def to_pair(group, shard, step):
        rows = pl.ds(shard * 16, 16)
        begin(remote(
            full1.at[group, rows], grads_ref.at[group, me["core"], rows], s7.at[group, step], r7.at[group, step], moved("core", 1)
        ))

    def spread_pair(group):
        axis = orders[group][0]
        for step in (1, 3, 2):
            block = full1.at[group, pl.ds(sender(axis, step) * 16, 16)]
            remote(block, block, s6.at[group, step - 1], r6.at[group, step - 1], moved(axis, step)).wait_recv()
            to_pair(group, sender(axis, step), step)
        keep = pltpu.make_async_copy(full1.at[group], grads_ref.at[group, me["core"]], local_s.at[8 + group])
        keep.start()
        locals_out.append(keep)

    def finish_pair(group):
        axis = orders[group][0]
        for step in range(4):
            rows = pl.ds(sender(axis, step) * 16, 16)
            remote(
                full1.at[group, rows], grads_ref.at[group, 1 - me["core"], rows], s7.at[group, step], r7.at[group, step], moved("core", 1)
            ).wait_recv()

    def give_back(at, values):
        back[at] = dot(scatter_ref[...], values).astype(BF16)
        arrived[at, 0, 0:48] = back[at, LR : LR + 48]
        arrived[at, 0, 48:128] = back[at, S1L : S1L + 80]
        arrived[at, 1, 128:288] = back[at, S2U : S2U + 160]
        routes = (
            (back.at[at, pl.ds(UR, 128)], arrived.at[at, 1, pl.ds(0, 128)], grid_moved(-1, 0)),
            (back.at[at, pl.ds(S2L, 160)], arrived.at[at, 0, pl.ds(128, 160)], grid_moved(1, 0)),
            (back.at[at, pl.ds(LL, 48)], arrived.at[at, 0, pl.ds(288, 48)], grid_moved(0, -1)),
            (back.at[at, pl.ds(UL, 48)], arrived.at[at, 1, pl.ds(288, 48)], grid_moved(-1, -1)),
        )
        return [
            begin(remote(src, dst, back_s.at[at, n], back_r.at[at, n], target))
            for n, (src, dst, target) in enumerate(routes)
        ]

    def take_back(at, arriving, out):
        for copy in arriving:
            copy.wait_recv()
        for half in range(2):
            rows = dot(unpack_ref[...], arrived[at, half]).astype(BF16)
            out_s[at, :, 3 * half : 3 * half + 3] = rows.reshape(LEVELS, 3, LONS, D)
        keep = pltpu.make_async_copy(out_s.at[at], out, local_s.at[12 + at])
        keep.start()
        locals_out.append(keep)

    def gain_copy(src, dst, sem, axis, step):
        return remote(src, dst, sg.at[sem], rg.at[sem], moved(axis, step))

    def gain_send(axis, buffer, value, first):
        own = buffer.at[me[axis]]
        own[...] = value
        for step in range(1, RING[axis]):
            begin(gain_copy(own, own, first + step, axis, step))

    def gain_take(axis, buffer, first):
        for step in range(1, RING[axis]):
            block = buffer.at[sender(axis, step)]
            gain_copy(block, block, first + step, axis, step).wait_recv()
        total = buffer[0]
        for at in range(1, RING[axis]):
            total = total + buffer[at]
        return total

    def backward(pair):
        for slot in range(4):
            rows = rows_of(slot)
            probs = probs_s[slot * 4 + pair]
            gm = gmix[rows, columns_of(0, pair)]
            grows[rows, columns_of(2, pair)] = unstack(dot(probs, gm)).astype(BF16)
            gprobs = dot_nt(stack(qkv[rows, columns_of(2, pair)]), gm).reshape(2, SPAN, SPAN)
            wide = probs.astype(F32).reshape(2, SPAN, SPAN)
            total = jnp.sum(wide * gprobs, 1, keepdims=True)
            gscores = (wide * (gprobs - total)).astype(BF16).reshape(2 * SPAN, SPAN)
            grows[rows, columns_of(0, pair)] = (dot_tn(gscores, stack(qkv[rows, columns_of(1, pair)])) * 0.125).astype(BF16)
            grows[rows, columns_of(1, pair)] = (unstack(dot(gscores, qkv[rows, columns_of(0, pair)])) * 0.125).astype(BF16)

    backward(0)
    reduce_pair(0)
    proj = dot(mixed[...], wout_ref[...]).astype(BF16)
    loads["scatter"].wait()
    lay_copies = give_back(0, (tokw[...].astype(F32) + proj.astype(F32)).astype(BF16))
    backward(1)
    reduce_pair(1)
    reduce_first(0)
    backward(2)
    reduce_pair(2)
    reduce_first(1)
    backward(3)
    reduce_pair(3)
    reduce_first(2)
    gnormed = dot_nt(grows[...], wqkv_ref[...]).astype(BF16).astype(F32)
    reduce_first(3)
    reduce_second(0)
    xhat = xhat_s[...]
    gain_rows = jnp.sum(gnormed * xhat, 0, keepdims=True)
    gain_own[...] = jnp.concatenate(
        [gain_rows[:, n * 128 : (n + 1) * 128] for n in range(4)] + [jnp.zeros((4, 128), F32)], 0
    )
    begin(gain_copy(gain_own, gain_core, 0, "core", 1))
    scaled = gnormed * gain_ref[...]
    gtok = cotw[...].astype(F32) + inv_s[...] * (
        scaled - jnp.mean(scaled, -1, keepdims=True) - xhat * jnp.mean(scaled * xhat, -1, keepdims=True)
    )
    reduce_second(1)
    gain_copy(gain_own, gain_core, 0, "core", 1).wait_recv()
    gain_send("x", gain_x, gain_own[...] + gain_core[...], 0)
    reduce_second(2)
    reduce_third(0)
    reduce_second(3)
    gain_send("y", gain_y, gain_take("x", gain_x, 0), 3)
    loads["unpack"].wait()
    take_back(0, lay_copies, lay_ref)
    reduce_third(1)
    spread_third(0)
    gain_send("z", gain_z, gain_take("y", gain_y, 3), 6)
    spread_third(1)
    gtok_copies = give_back(1, gtok.astype(BF16))
    spread_second(0)
    spread_second(1)
    spread_first(0)
    spread_first(1)
    spread_first(2)
    spread_first(3)
    ggain_ref[...] = gain_take("z", gain_z, 6) * factor
    spread_pair(0)
    spread_pair(1)
    take_back(1, gtok_copies, gtok_ref)
    spread_pair(2)
    spread_pair(3)
    for group in range(4):
        finish_pair(group)
    for copy in locals_out:
        copy.wait()
    for copy in pending:
        copy.wait_send()


def unpack_kernel(lay_in, gtok_in, grads_in, gain_in, lay_out, gtok_out, gqkv_out, gout_out, gain_out, narrow, wide, last, grids, sems):
    moves = [pltpu.make_async_copy(grads_in.at[group], narrow.at[group], sems.at[group]) for group in range(4)]
    moves += [pltpu.make_async_copy(source, grids.at[at], sems.at[4 + at]) for at, source in enumerate((lay_in, gtok_in))]
    outs = []
    for at in (4, 5, 0, 1, 2, 3):
        moves[at].start()
    for n in range(4):
        gain_out[:, n * 128 : (n + 1) * 128] = gain_in[n : n + 1]
    for at, target in enumerate((lay_out, gtok_out)):
        moves[4 + at].wait()
        outs.append(pltpu.make_async_copy(grids.at[at], target, sems.at[10 + at]))
        outs[-1].start()
    for group in range(4):
        moves[group].wait()
        for part in range(3):
            tiles = narrow[group, part // 2, (part % 2) * 32 : (part % 2 + 1) * 32]
            columns = pl.ds(part * D + group * 128, 128)
            wide[:, columns] = tiles.astype(F32).reshape(D, 128)
            outs.append(pltpu.make_async_copy(wide.at[:, columns], gqkv_out.at[:, columns], sems.at[12 + group * 3 + part]))
            outs[-1].start()
        for n in range(4):
            tiles = narrow[group, 1, 32 + n * 8 : 32 + (n + 1) * 8]
            last[group * 128 : (group + 1) * 128, n * 128 : (n + 1) * 128] = tiles.astype(F32).reshape(128, 128)
        rows = pl.ds(group * 128, 128)
        outs.append(pltpu.make_async_copy(last.at[rows], gout_out.at[rows], sems.at[6 + group]))
        outs[-1].start()
    for copy in outs:
        copy.wait()


def on_device(tokens, cotangent, norm_gain, qkv_weight, out_weight):
    pack = packing()
    tables = [jnp.asarray(table, BF16) for table in (pack, pack.T, gathering(), scattering())]
    vmem = pl.BlockSpec(memory_space=pltpu.VMEM)
    anywhere = pl.BlockSpec(memory_space=pl.ANY)
    dma = pltpu.SemaphoreType.DMA
    rows = 4 * SPAN
    scratch = [
        pltpu.VMEM(tokens.shape, BF16),
        pltpu.VMEM(tokens.shape, BF16),
        pltpu.VMEM((D, 3 * D), BF16),
        pltpu.VMEM((D, D), BF16),
        *[pltpu.VMEM(table.shape, BF16) for table in tables],
        pltpu.VMEM((2, *tokens.shape), BF16),
        pltpu.VMEM((2, 2, PACKED, D), BF16),
        pltpu.VMEM((2, STAGED, D), BF16),
        pltpu.VMEM((2, STAGED, D), BF16),
        pltpu.VMEM((2, 2, PACKED, D), BF16),
        pltpu.VMEM((rows, D), F32),
        pltpu.VMEM((rows, 1), F32),
        pltpu.VMEM((rows, D), BF16),
        pltpu.VMEM((rows, D), BF16),
        pltpu.VMEM((rows, D), BF16),
        pltpu.VMEM((rows, 3 * D), BF16),
        pltpu.VMEM((rows, D), BF16),
        pltpu.VMEM((16, 2 * SPAN, SPAN), BF16),
        pltpu.VMEM((rows, D), BF16),
        pltpu.VMEM((rows, 3 * D), BF16),
        pltpu.VMEM((4, 64, 16, 128), BF16),
        pltpu.VMEM((4, 64, 16, 128), BF16),
        pltpu.VMEM((4, 64, 16, 128), F32),
        pltpu.VMEM((4, 64, 16, 128), BF16),
        pltpu.VMEM((4, 3, 16, 16, 128), BF16),
        pltpu.VMEM((4, 16, 16, 128), F32),
        pltpu.VMEM((4, 16, 16, 128), BF16),
        pltpu.VMEM((4, 3, 4, 16, 128), BF16),
        pltpu.VMEM((2, 8, 16, 128), F32),
        pltpu.VMEM((2, 8, 16, 128), BF16),
        pltpu.VMEM((2, 7, 16, 128), BF16),
        pltpu.VMEM((2, 8, 16, 128), BF16),
        pltpu.VMEM((4, 64, 16, 128), BF16),
        pltpu.VMEM((8, 128), F32),
        pltpu.VMEM((8, 128), F32),
        pltpu.VMEM((4, 8, 128), F32),
        pltpu.VMEM((4, 8, 128), F32),
        pltpu.VMEM((8, 8, 128), F32),
        dma((14,)),
        dma((2, 6)), dma((2, 6)), dma((2, 4)), dma((2, 4)),
        dma((4,)), dma((4,)),
        dma((4, 3)), dma((4, 3)),
        dma((4, 3)), dma((4, 3)),
        dma((2, 7)), dma((2, 7)),
        dma((2, 7)), dma((2, 7)),
        dma((4, 3)), dma((4, 3)),
        dma((4, 3)), dma((4, 3)),
        dma((4, 4)), dma((4, 4)),
        dma((14,)), dma((14,)),
    ]
    grid = jax.ShapeDtypeStruct(tokens.shape, BF16)
    parts = pl.pallas_call(
        kernel,
        out_shape=(
            grid,
            grid,
            jax.ShapeDtypeStruct((4, 2, 64, 16, 128), BF16),
            jax.ShapeDtypeStruct((8, 128), F32),
        ),
        in_specs=[anywhere, anywhere, vmem] + [anywhere] * 6,
        out_specs=(anywhere, anywhere, anywhere, vmem),
        scratch_shapes=scratch,
        compiler_params=pltpu.CompilerParams(
            collective_id=0, has_side_effects=True, vmem_limit_bytes=56 * 1024 * 1024
        ),
        name="sublayer",
    )(tokens, cotangent, norm_gain.reshape(1, D), qkv_weight, out_weight, *tables)
    layer_out, grad_tokens, grad_qkv, grad_out, grad_gain = pl.pallas_call(
        unpack_kernel,
        out_shape=(
            grid,
            grid,
            jax.ShapeDtypeStruct((D, 3 * D), F32),
            jax.ShapeDtypeStruct((D, D), F32),
            jax.ShapeDtypeStruct((1, D), F32),
        ),
        in_specs=[anywhere] * 3 + [vmem],
        out_specs=(anywhere,) * 4 + (vmem,),
        scratch_shapes=[pltpu.VMEM((4, 2, 64, 16, 128), BF16), pltpu.VMEM((D, 3 * D), F32), pltpu.VMEM((D, D), F32), pltpu.VMEM((2, *tokens.shape), BF16), dma((24,))],
        compiler_params=pltpu.CompilerParams(vmem_limit_bytes=60 * 1024 * 1024),
        name="results",
    )(*parts)
    return layer_out, grad_tokens, grad_qkv, grad_out, grad_gain.reshape(D)


def solution(mesh):
    grid = P(None, "lat", "lon", None)
    return jax.shard_map(
        on_device,
        mesh=mesh,
        in_specs=(grid, grid, P(), P(), P()),
        out_specs=(grid, grid, P(), P(), P()),
        check_vma=False,
    )
```
